32 devices in a mesh: groups: 2 (over x), seq: 16 (over z, y, core).
Axes of the slice: x: 2, y: 2, z: 4, core: 2. Of those that a mesh axis runs over, the one named last changes fastest.
Arguments:
- queries: bfloat16 [256, 2560], P(('groups', 'seq')), parts along dimension 0, may hold values from -130 to 130
- cache_keys: bfloat16 [32768, 2560], P(('groups', 'seq')), parts along dimension 0, may hold values from -6 to 6
- cache_values: bfloat16 [32768, 2560], P(('groups', 'seq')), parts along dimension 0, may hold values from -6 to 6
- span_keys: bfloat16 [256, 2560], P(('groups', 'seq')), parts along dimension 0, may hold values from -8 to 8
- span_values: bfloat16 [256, 2560], P(('groups', 'seq')), parts along dimension 0, may hold values from -6 to 6
- cache_tokens: int32 [2], P('groups'), parts along dimension 0, may hold values from 8192 to 16384
- span_start: int32 [2], P('groups'), parts along dimension 0, may hold values from 1433 to 1559
Outputs:
- attended: bfloat16 [256, 2560], P(('groups', 'seq')), parts along dimension 0
The draws below stay inside these ranges and needn't reach their ends.
There are 2 independent parts, one for each index of `groups`. The reference program is written for one: setup_inputs(seed, part) draws one part's arguments, and reference() takes and returns one part's arrays. A program takes and returns all parts, laid end to end along the dimension named above; each array names one. Nothing has to cross between parts.
All inputs are finite; a program needn't handle non-finite values.
Results may differ from the reference program's by a relative error of at most 0.0026.
Values may be sent and summed in bfloat16 or wider, within the bound.
A program may use at most 320 MiB of HBM per device.

```python
import math
import jax
import jax.numpy as jnp
from jax import lax

HEAD_DIM = 128
HEADS = 20
FRAME_TOK = 1560
CDEV = 1024
SPAN = 128
CACHE = 16384
N_SEQ = 16


def draw_queries(key, part):
    sample = 3.0 * jax.random.truncated_normal(jax.random.fold_in(key, 1), -6.0, 6.0, (SPAN, HEADS * HEAD_DIM), jnp.float32)
    return sample.astype(jnp.bfloat16)


def draw_cache_keys(key, part):
    sample = jax.random.truncated_normal(jax.random.fold_in(key, 2), -6.0, 6.0, (CACHE, HEADS * HEAD_DIM), jnp.float32)
    return sample.astype(jnp.bfloat16)


def block_levels(rng, dims, pieces, low, largest):
    def one(dim, shards_of):
        steps = jax.random.uniform(jax.random.fold_in(jax.random.fold_in(rng, 6), dim), (shards_of,), jnp.float32, low / len(pieces), largest / len(pieces))
        return jnp.repeat(jnp.exp(steps), dims[dim] // shards_of).reshape((-1,) + (1,) * (len(dims) - dim - 1))

    factor_of = one(*pieces[0])
    for cut in pieces[1:]:
        factor_of = factor_of * one(*cut)
    return factor_of


def bell_draw(stream_key, shape, spread, bound, cuts=(), kind=jnp.bfloat16):
    drawn = jax.random.normal(stream_key, shape, jnp.float32) * spread
    if len(cuts) > 0:
        drawn = block_levels(stream_key, shape, cuts, -0.22, 0.18) * drawn
    return jnp.clip(drawn, min=-bound, max=bound).astype(kind)


def setup_inputs(seed: int = 0, part: int = 0) -> dict:
    splits = jax.random.split(jax.random.key(seed), 8)
    part_splits = jax.random.split(jax.random.fold_in(splits[7], part), 8)
    queries = draw_queries(jax.random.fold_in(jax.random.fold_in(splits[7], part), 71), part)
    cache_keys = draw_cache_keys(jax.random.fold_in(jax.random.fold_in(splits[7], part), 71), part)
    cache_values = bell_draw(part_splits[2], (CACHE, HEADS * HEAD_DIM), 1.0, 6.0, ((0, 16),))
    span_keys = bell_draw(part_splits[3], (SPAN, HEADS * HEAD_DIM), 1.3, 8.0, ((0, 16),))
    span_values = bell_draw(part_splits[4], (SPAN, HEADS * HEAD_DIM), 1.0, 6.0, ((0, 16),))
    cache_tokens = jax.random.randint(part_splits[5], (1,), CACHE // 2, CACHE + 1).astype(jnp.int32)
    span_start = jax.random.randint(part_splits[6], (1,), FRAME_TOK - SPAN + 1, FRAME_TOK).astype(jnp.int32)
    return dict(queries=queries, cache_keys=cache_keys, cache_values=cache_values, span_keys=span_keys, span_values=span_values, cache_tokens=cache_tokens, span_start=span_start)


NEG_FILL = -1e+30

def reference(queries, cache_keys, cache_values, span_keys, span_values, cache_tokens, span_start):
    score_scale = 1.0 / math.sqrt(HEAD_DIM)
    query_heads = queries.astype(jnp.float32).reshape(SPAN, HEADS, HEAD_DIM)
    valid_end = cache_tokens[0]
    frame_of = (span_start[0] + jnp.arange(SPAN, dtype=jnp.int32)) // FRAME_TOK
    span_mask = frame_of[None, :] <= frame_of[:, None]
    own_keys = span_keys.astype(jnp.float32).reshape(SPAN, HEADS, HEAD_DIM)
    own_values = span_values.astype(jnp.float32).reshape(SPAN, HEADS, HEAD_DIM)
    span_scores = jnp.einsum('qhd,khd->hqk', query_heads, own_keys) * score_scale
    span_scores = jnp.where(span_mask[None], span_scores, NEG_FILL)
    key_blocks = cache_keys.reshape(N_SEQ, CDEV, HEADS, HEAD_DIM)
    value_blocks = cache_values.reshape(N_SEQ, CDEV, HEADS, HEAD_DIM)
    offsets = jnp.arange(N_SEQ, dtype=jnp.int32) * CDEV

    def block_scores(key_rows, offset):
        scores = jnp.einsum('qhd,khd->hqk', query_heads, key_rows.astype(jnp.float32)) * score_scale
        position = offset + jnp.arange(CDEV, dtype=jnp.int32)
        return jnp.where((position < valid_end)[None, None, :], scores, NEG_FILL)

    def max_step(running, block_item):
        key_rows, offset = block_item
        return (jnp.maximum(running, lax.optimization_barrier(jnp.max(block_scores(key_rows, offset), axis=2))), None)
    row_top, _ = lax.scan(max_step, lax.optimization_barrier(jnp.max(span_scores, axis=2)), (key_blocks, offsets))

    def weigh(scores, value_rows):
        weights = jnp.exp(scores - row_top[:, :, None])
        rounded = lax.optimization_barrier(weights.astype(jnp.bfloat16)).astype(jnp.float32)
        return (lax.optimization_barrier(jnp.sum(weights, axis=2)), jnp.einsum('hqk,khd->qhd', rounded, value_rows.astype(jnp.float32)))
    first_den, first_num = weigh(span_scores, own_values)

    def sum_step(running, block_item):
        key_rows, value_rows, offset = block_item
        part_den, part_num = weigh(block_scores(key_rows, offset), value_rows)
        return ((running[0] + part_den, running[1] + part_num), None)
    (denominator, numerator), _ = lax.scan(sum_step, (first_den, first_num), (key_blocks, value_blocks, offsets))
    attended = numerator / jnp.transpose(denominator)[:, :, None]
    return attended.reshape(SPAN, HEADS * HEAD_DIM).astype(jnp.bfloat16)
```

```python
import functools
import math

import jax
import jax.numpy as jnp
from jax import lax
from jax.experimental import pallas as pl
from jax.experimental.pallas import tpu as pltpu
from jax.sharding import PartitionSpec as P

HEAD_DIM = 128
FRAME_TOK = 1560
NEG_FILL = -1e30
LANES = 128
MESH = pl.DeviceIdType.MESH


def merge(x, y, heads):
    width = heads * HEAD_DIM
    sx, sy = x[:, width:], y[:, width:]
    top = jnp.maximum(sx, sy)
    fx, fy = jnp.exp2(sx - top), jnp.exp2(sy - top)
    lane = lax.broadcasted_iota(jnp.int32, sx.shape, 1)
    den = sx * pltpu.roll(fx, 64, 1) + sy * pltpu.roll(fy, 64, 1)
    pieces = []
    for j in range(heads):
        cut = slice(j * HEAD_DIM, (j + 1) * HEAD_DIM)
        pieces.append(x[:, cut] * fx[:, j : j + 1] + y[:, cut] * fy[:, j : j + 1])
    pieces.append(jnp.where(lane < 64, top, den))
    return jnp.concatenate(pieces, axis=1)


def kernel(
    n, chunks,
    tok_ref, start_ref, q_ref, k_hbm, v_hbm, sk_ref, sv_ref, o_ref,
    qg, kbuf, vbuf, part, ra, rb, rc, bias_row, bias_span,
    kv_sem, g_send, g_recv, a_send, a_recv, b_send, b_recv, c_send, c_recv,
):
    rows, width = k_hbm.shape
    own = q_ref.shape[0]
    chips = n // 2
    far = chips // 2
    total = n * own
    heads = width // HEAD_DIM // chunks
    cw = heads * HEAD_DIM
    cs = cw + LANES
    coef = math.log2(math.e) / math.sqrt(HEAD_DIM)

    me = lax.axis_index("seq")
    group = lax.axis_index("groups")
    core = lax.rem(me, 2)
    side = lax.rem(me // 2, 2)
    hi = me // 4

    def device(hi_, side_, core_):
        return (group, (hi_ * 2 + side_) * 2 + core_)

    def slot_of(hi_, side_, core_):
        return core_ * chips + side_ * far + hi_

    sibling = device(hi, side, 1 - core)
    across = device(hi, 1 - side, core)

    def kv_copy(c, which):
        cut = pl.ds(pl.multiple_of(c * cw, LANES), cw)
        src, dst = (k_hbm, kbuf) if which == 0 else (v_hbm, vbuf)
        return pltpu.make_async_copy(
            src.at[:, cut], dst.at[pl.ds(0, rows), cut], kv_sem.at[which, c]
        )

    for c in range(chunks):
        kv_copy(c, 0).start()
        kv_copy(c, 1).start()

    barrier = pltpu.get_barrier_semaphore()
    pl.semaphore_signal(barrier, inc=1, device_id=sibling, device_id_type=MESH)
    pl.semaphore_signal(barrier, inc=1, device_id=across, device_id_type=MESH)
    for d in range(1, far):
        pl.semaphore_signal(
            barrier, inc=1, device_id=device(lax.rem(hi + d, far), side, core), device_id_type=MESH
        )

    my_slot = slot_of(hi, side, core)
    qg[pl.ds(my_slot, 1)] = q_ref[...][None]

    pl.semaphore_wait(barrier, far + 1)

    def gather_copy(slot, to, number):
        return pltpu.make_async_remote_copy(
            src_ref=qg.at[slot], dst_ref=qg.at[slot],
            send_sem=g_send.at[number], recv_sem=g_recv.at[slot],
            device_id=to, device_id_type=MESH,
        )

    sends = []

    def gather_send(slot, to):
        copy = gather_copy(slot, to, len(sends))
        copy.start()
        sends.append(copy)

    def gather_wait(slot):
        gather_copy(slot, sibling, 0).wait_recv()

    for d in range(1, far):
        gather_send(my_slot, device(lax.rem(hi + d, far), side, core))
    gather_send(my_slot, across)
    gather_send(my_slot, sibling)

    position = me * rows + lax.broadcasted_iota(jnp.int32, bias_row.shape, 1)
    bias_row[...] = jnp.where(position < tok_ref[0], 0.0, NEG_FILL)
    shape = (total, LANES)
    row = lax.broadcasted_iota(jnp.int32, shape, 0)
    lane = lax.broadcasted_iota(jnp.int32, shape, 1)
    token = row
    for s in range(n):
        s_core, s_side, s_hi = s // chips, (s % chips) // far, s % far
        owner = (s_hi * 2 + s_side) * 2 + s_core
        inside = jnp.logical_and(row >= s * own, row < (s + 1) * own)
        token = jnp.where(inside, row + (owner - s) * own, token)
    key = me * own + lane
    seen = lane < own
    for f in range(1, (FRAME_TOK - 1 + total) // FRAME_TOK + 1):
        edge = f * FRAME_TOK - start_ref[0]
        seen = jnp.logical_and(seen, jnp.logical_or(key < edge, token >= edge))
    bias_span[...] = jnp.where(seen, 0.0, NEG_FILL)
    pad = jnp.zeros((LANES - own, width), jnp.float32)
    for ref, buf in ((sk_ref, kbuf), (sv_ref, vbuf)):
        block = jnp.concatenate([ref[...].astype(jnp.float32), pad], axis=0)
        buf[pl.ds(rows, LANES), :] = block.astype(jnp.bfloat16)

    for d in range(1, far):
        slot = slot_of(lax.rem(hi - d + far, far), side, core)
        gather_wait(slot)
        gather_send(slot, across)
        gather_send(slot, sibling)
    for d in range(far):
        slot = slot_of(lax.rem(hi - d + far, far), 1 - side, core)
        gather_wait(slot)
        gather_send(slot, sibling)
    for s_side in (side, 1 - side):
        for d in range(far):
            gather_wait(slot_of(lax.rem(hi - d + far, far), s_side, 1 - core))

    def a_copy(c):
        return pltpu.make_async_remote_copy(
            src_ref=part.at[c, pl.ds((1 - core) * chips, chips)], dst_ref=ra.at[c],
            send_sem=a_send.at[c], recv_sem=a_recv.at[c],
            device_id=sibling, device_id_type=MESH,
        )

    def b_copy(c):
        return pltpu.make_async_remote_copy(
            src_ref=part.at[c, pl.ds(core * chips + (1 - side) * far, far)], dst_ref=rb.at[c],
            send_sem=b_send.at[c], recv_sem=b_recv.at[c],
            device_id=across, device_id_type=MESH,
        )

    def c_copy(c, d):
        other = lax.rem(hi + d, far)
        return pltpu.make_async_remote_copy(
            src_ref=part.at[c, slot_of(other, side, core)], dst_ref=rc.at[c, d - 1],
            send_sem=c_send.at[c, d - 1], recv_sem=c_recv.at[c, d - 1],
            device_id=device(other, side, core), device_id_type=MESH,
        )

    def attend(c):
        kv_copy(c, 0).wait()
        kv_copy(c, 1).wait()
        stat_lane = lax.broadcasted_iota(jnp.int32, (total, LANES), 1)
        stats = jnp.zeros((total, LANES), jnp.float32)
        for j in range(heads):
            cut = pl.ds(pl.multiple_of(c * cw + j * HEAD_DIM, LANES), HEAD_DIM)
            q = qg[:, :, cut].astype(jnp.float32).reshape(total, HEAD_DIM).astype(jnp.bfloat16)
            s = lax.dot_general(
                q, kbuf[:, cut], (((1,), (1,)), ((), ())), preferred_element_type=jnp.float32
            ) * coef
            s_cache = s[:, :rows] + bias_row[...]
            s_span = s[:, rows:] + bias_span[...]
            s = jnp.concatenate([s_cache, s_span], axis=1)
            top = jnp.max(s, axis=1, keepdims=True)
            w = jnp.exp2(s - top)
            den = jnp.sum(w, axis=1, keepdims=True)
            high = w.astype(jnp.bfloat16)
            low = (w - high.astype(jnp.float32)).astype(jnp.bfloat16)
            both = jnp.dot(
                jnp.concatenate([high, low], axis=0), vbuf[:, cut],
                preferred_element_type=jnp.float32,
            )
            num = both[:total] + both[total:]
            part[c, :, :, j * HEAD_DIM : (j + 1) * HEAD_DIM] = num.reshape(n, own, HEAD_DIM)
            stats = jnp.where(stat_lane == j, top, stats)
            stats = jnp.where(stat_lane == 64 + j, den, stats)
        part[c, :, :, cw:] = stats.reshape(n, own, LANES)

    def merge_a(c):
        a_copy(c).wait_recv()
        mine = pl.ds(core * chips, chips)
        x = part[c, mine].reshape(chips * own, cs)
        y = ra[c].reshape(chips * own, cs)
        part[c, mine] = merge(x, y, heads).reshape(chips, own, cs)
        b_copy(c).start()

    def merge_b(c):
        b_copy(c).wait_recv()
        mine = pl.ds(core * chips + side * far, far)
        x = part[c, mine].reshape(far * own, cs)
        y = rb[c].reshape(far * own, cs)
        part[c, mine] = merge(x, y, heads).reshape(far, own, cs)
        for d in range(1, far):
            c_copy(c, d).start()

    def finish(c):
        x = part[c, my_slot]
        for d in range(1, far):
            c_copy(c, d).wait_recv()
            x = merge(x, rc[c, d - 1], heads)
        out = [
            x[:, j * HEAD_DIM : (j + 1) * HEAD_DIM] / x[:, cw + 64 + j : cw + 65 + j]
            for j in range(heads)
        ]
        cut = pl.ds(pl.multiple_of(c * cw, LANES), cw)
        o_ref[:, cut] = jnp.concatenate(out, axis=1).astype(jnp.bfloat16)

    def step(t, _):
        @pl.when(t < chunks)
        def _():
            attend(t)
            a_copy(t).start()

        @pl.when(jnp.logical_and(t >= 1, t < chunks + 1))
        def _():
            merge_a(t - 1)

        @pl.when(jnp.logical_and(t >= 2, t < chunks + 2))
        def _():
            merge_b(t - 2)

        @pl.when(t >= 3)
        def _():
            finish(t - 3)

        return 0

    lax.fori_loop(0, chunks + 3, step, 0)

    for copy in sends:
        copy.wait_send()
    for c in range(chunks):
        a_copy(c).wait_send()
        b_copy(c).wait_send()
        for d in range(1, far):
            c_copy(c, d).wait_send()


def local(n, queries, cache_keys, cache_values, span_keys, span_values, cache_tokens, span_start):
    own, width = queries.shape
    rows = cache_keys.shape[0]
    heads = width // HEAD_DIM
    chunks = 4 if heads % 4 == 0 else 1
    chips = n // 2
    far = chips // 2
    total = n * own
    cs = width // chunks + LANES
    smem = pl.BlockSpec(memory_space=pltpu.SMEM)
    vmem = pl.BlockSpec(memory_space=pltpu.VMEM)
    hbm = pl.BlockSpec(memory_space=pl.ANY)
    dma = pltpu.SemaphoreType.DMA
    return pl.pallas_call(
        functools.partial(kernel, n, chunks),
        out_shape=jax.ShapeDtypeStruct((own, width), jnp.bfloat16),
        in_specs=[smem, smem, vmem, hbm, hbm, vmem, vmem],
        out_specs=vmem,
        scratch_shapes=[
            pltpu.VMEM((n, own, width), jnp.bfloat16),
            pltpu.VMEM((rows + LANES, width), jnp.bfloat16),
            pltpu.VMEM((rows + LANES, width), jnp.bfloat16),
            pltpu.VMEM((chunks, n, own, cs), jnp.float32),
            pltpu.VMEM((chunks, chips, own, cs), jnp.float32),
            pltpu.VMEM((chunks, far, own, cs), jnp.float32),
            pltpu.VMEM((chunks, far - 1, own, cs), jnp.float32),
            pltpu.VMEM((1, rows), jnp.float32),
            pltpu.VMEM((total, LANES), jnp.float32),
            dma((2, chunks)),
            dma((far - 1 + far + chips,)),
            dma((n,)),
            dma((chunks,)),
            dma((chunks,)),
            dma((chunks,)),
            dma((chunks,)),
            dma((chunks, far - 1)),
            dma((chunks, far - 1)),
        ],
        compiler_params=pltpu.CompilerParams(
            collective_id=0, has_side_effects=True, vmem_limit_bytes=56 * 1024 * 1024
        ),
    )(cache_tokens, span_start, queries, cache_keys, cache_values, span_keys, span_values)


def solution(mesh):
    placed = (
        P(("groups", "seq"), None),
        P(("groups", "seq"), None),
        P(("groups", "seq"), None),
        P(("groups", "seq"), None),
        P(("groups", "seq"), None),
        P("groups"),
        P("groups"),
    )
    return jax.shard_map(
        functools.partial(local, mesh.shape["seq"]),
        mesh=mesh, in_specs=placed, out_specs=P(("groups", "seq"), None), check_vma=False,
    )
```

```python
import functools
import math

import jax
import jax.numpy as jnp
from jax import lax
from jax.experimental import pallas as pl
from jax.experimental.pallas import tpu as pltpu
from jax.sharding import PartitionSpec as P

HEAD_DIM = 128
FRAME_TOK = 1560
NEG_FILL = -1e30
LANES = 128
MESH = pl.DeviceIdType.MESH


def merge(x, y, heads):
    width = heads * HEAD_DIM
    sx, sy = x[:, width:], y[:, width:]
    top = jnp.maximum(sx, sy)
    fx, fy = jnp.exp2(sx - top), jnp.exp2(sy - top)
    lane = lax.broadcasted_iota(jnp.int32, sx.shape, 1)
    den = sx * pltpu.roll(fx, 64, 1) + sy * pltpu.roll(fy, 64, 1)
    pieces = []
    for j in range(heads):
        cut = slice(j * HEAD_DIM, (j + 1) * HEAD_DIM)
        pieces.append(x[:, cut] * fx[:, j : j + 1] + y[:, cut] * fy[:, j : j + 1])
    pieces.append(jnp.where(lane < 64, top, den))
    return jnp.concatenate(pieces, axis=1)


def kernel(
    n, chunks,
    tok_ref, start_ref, q_ref, k_hbm, v_hbm, sk_ref, sv_ref, o_ref,
    qg, kbuf, vbuf, part, ra, rb, rc, bias_row, bias_span,
    kv_sem, g_send, g_recv, a_send, a_recv, b_send, b_recv, c_send, c_recv,
):
    rows, width = k_hbm.shape
    own = q_ref.shape[0]
    chips = n // 2
    far = chips // 2
    total = n * own
    heads = width // HEAD_DIM // chunks
    cw = heads * HEAD_DIM
    cs = cw + LANES
    coef = math.log2(math.e) / math.sqrt(HEAD_DIM)

    me = lax.axis_index("seq")
    group = lax.axis_index("groups")
    core = lax.rem(me, 2)
    side = lax.rem(me // 2, 2)
    hi = me // 4

    def device(hi_, side_, core_):
        return (group, (hi_ * 2 + side_) * 2 + core_)

    def slot_of(hi_, side_, core_):
        return core_ * chips + side_ * far + hi_

    sibling = device(hi, side, 1 - core)
    across = device(hi, 1 - side, core)

    def kv_copy(c, which):
        cut = pl.ds(pl.multiple_of(c * cw, LANES), cw)
        src, dst = (k_hbm, kbuf) if which == 0 else (v_hbm, vbuf)
        return pltpu.make_async_copy(
            src.at[:, cut], dst.at[pl.ds(0, rows), cut], kv_sem.at[which, c]
        )

    for c in range(chunks):
        kv_copy(c, 0).start()
        kv_copy(c, 1).start()

    barrier = pltpu.get_barrier_semaphore()
    pl.semaphore_signal(barrier, inc=1, device_id=sibling, device_id_type=MESH)
    pl.semaphore_signal(barrier, inc=1, device_id=across, device_id_type=MESH)
    for d in range(1, far):
        pl.semaphore_signal(
            barrier, inc=1, device_id=device(lax.rem(hi + d, far), side, core), device_id_type=MESH
        )

    my_slot = slot_of(hi, side, core)
    for c in range(chunks):
        qg[c, pl.ds(my_slot, 1)] = q_ref[:, c * cw : (c + 1) * cw][None]

    pl.semaphore_wait(barrier, far + 1)

    def gather_copy(c, slot, to, number):
        return pltpu.make_async_remote_copy(
            src_ref=qg.at[c, slot], dst_ref=qg.at[c, slot],
            send_sem=g_send.at[c, number], recv_sem=g_recv.at[c, slot],
            device_id=to, device_id_type=MESH,
        )

    def from_behind(d):
        return lax.rem(hi - d + far, far)

    def gather_own(c):
        for d in range(1, far):
            to = device(lax.rem(hi + d, far), side, core)
            gather_copy(c, my_slot, to, d - 1).start()
        gather_copy(c, my_slot, across, far - 1).start()
        gather_copy(c, my_slot, sibling, 2 * far - 1).start()

    def gather_far(c):
        for d in range(1, far):
            slot = slot_of(from_behind(d), side, core)
            gather_copy(c, slot, sibling, 0).wait_recv()
            gather_copy(c, slot, across, far - 1 + d).start()
            gather_copy(c, slot, sibling, 2 * far - 1 + d).start()

    def gather_across(c):
        for d in range(far):
            slot = slot_of(from_behind(d), 1 - side, core)
            gather_copy(c, slot, sibling, 0).wait_recv()
            gather_copy(c, slot, sibling, 3 * far - 1 + d).start()

    def gather_sibling(c):
        for s_side in (side, 1 - side):
            for d in range(far):
                slot = slot_of(from_behind(d), s_side, 1 - core)
                gather_copy(c, slot, sibling, 0).wait_recv()

    for c in range(chunks):
        gather_own(c)

    position = me * rows + lax.broadcasted_iota(jnp.int32, bias_row.shape, 1)
    bias_row[...] = jnp.where(position < tok_ref[0], 0.0, NEG_FILL)
    shape = (total, LANES)
    row = lax.broadcasted_iota(jnp.int32, shape, 0)
    lane = lax.broadcasted_iota(jnp.int32, shape, 1)
    token = row
    for s in range(n):
        s_core, s_side, s_hi = s // chips, (s % chips) // far, s % far
        owner = (s_hi * 2 + s_side) * 2 + s_core
        inside = jnp.logical_and(row >= s * own, row < (s + 1) * own)
        token = jnp.where(inside, row + (owner - s) * own, token)
    key = me * own + lane
    seen = lane < own
    for f in range(1, (FRAME_TOK - 1 + total) // FRAME_TOK + 1):
        edge = f * FRAME_TOK - start_ref[0]
        seen = jnp.logical_and(seen, jnp.logical_or(key < edge, token >= edge))
    seen_bias = jnp.where(seen, 0.0, NEG_FILL)
    bias_span[pl.ds(0, total)] = seen_bias
    bias_span[pl.ds(total, total)] = seen_bias
    pad = jnp.zeros((LANES - own, width), jnp.float32)
    for ref, buf in ((sk_ref, kbuf), (sv_ref, vbuf)):
        block = jnp.concatenate([ref[...].astype(jnp.float32), pad], axis=0)
        buf[pl.ds(rows, LANES), :] = block.astype(jnp.bfloat16)

    gather_far(0)
    gather_across(0)
    if chunks > 1:
        gather_far(1)
    gather_sibling(0)

    def a_copy(c):
        return pltpu.make_async_remote_copy(
            src_ref=part.at[c, pl.ds((1 - core) * chips, chips)], dst_ref=ra.at[c],
            send_sem=a_send.at[c], recv_sem=a_recv.at[c],
            device_id=sibling, device_id_type=MESH,
        )

    def b_copy(c):
        return pltpu.make_async_remote_copy(
            src_ref=part.at[c, pl.ds(core * chips + (1 - side) * far, far)], dst_ref=rb.at[c],
            send_sem=b_send.at[c], recv_sem=b_recv.at[c],
            device_id=across, device_id_type=MESH,
        )

    def c_copy(c, d):
        other = lax.rem(hi + d, far)
        return pltpu.make_async_remote_copy(
            src_ref=part.at[c, slot_of(other, side, core)], dst_ref=rc.at[c, d - 1],
            send_sem=c_send.at[c, d - 1], recv_sem=c_recv.at[c, d - 1],
            device_id=device(other, side, core), device_id_type=MESH,
        )

    def attend(c, pair, stats):
        begin = pair * 2 * HEAD_DIM
        cut = pl.ds(pl.multiple_of(c * cw + begin, LANES), 2 * HEAD_DIM)
        q = qg[c, :, :, begin : begin + 2 * HEAD_DIM].astype(jnp.float32)
        q = q.reshape(total, 2 * HEAD_DIM)
        first = lax.broadcasted_iota(jnp.int32, q.shape, 1) < HEAD_DIM
        q = jnp.concatenate([jnp.where(first, q, 0.0), jnp.where(first, 0.0, q)], axis=0)
        s = lax.dot_general(
            q.astype(jnp.bfloat16), kbuf[:, cut], (((1,), (1,)), ((), ())),
            preferred_element_type=jnp.float32,
        ) * coef
        s_cache = s[:, :rows] + bias_row[...]
        s_span = s[:, rows:] + bias_span[...]
        s = jnp.concatenate([s_cache, s_span], axis=1)
        top = jnp.max(s, axis=1, keepdims=True)
        w = jnp.exp2(s - top)
        den = jnp.sum(w, axis=1, keepdims=True)
        num = jnp.dot(w.astype(jnp.bfloat16), vbuf[:, cut], preferred_element_type=jnp.float32)
        stat_lane = lax.broadcasted_iota(jnp.int32, (total, LANES), 1)
        for i in range(2):
            j, own_rows = 2 * pair + i, slice(i * total, (i + 1) * total)
            piece = num[own_rows, i * HEAD_DIM : (i + 1) * HEAD_DIM]
            part[c, :, :, j * HEAD_DIM : (j + 1) * HEAD_DIM] = piece.reshape(n, own, HEAD_DIM)
            stats = jnp.where(stat_lane == j, top[own_rows], stats)
            stats = jnp.where(stat_lane == 64 + j, den[own_rows], stats)
        part[c, :, :, cw:] = stats.reshape(n, own, LANES)
        return stats

    def merge_a(c):
        a_copy(c).wait_recv()
        mine = pl.ds(core * chips, chips)
        x = part[c, mine].reshape(chips * own, cs)
        y = ra[c].reshape(chips * own, cs)
        part[c, mine] = merge(x, y, heads).reshape(chips, own, cs)
        b_copy(c).start()

    def merge_b(c):
        b_copy(c).wait_recv()
        mine = pl.ds(core * chips + side * far, far)
        x = part[c, mine].reshape(far * own, cs)
        y = rb[c].reshape(far * own, cs)
        part[c, mine] = merge(x, y, heads).reshape(far, own, cs)
        for d in range(1, far):
            c_copy(c, d).start()

    def finish(c):
        x = part[c, my_slot]
        for d in range(1, far):
            c_copy(c, d).wait_recv()
            x = merge(x, rc[c, d - 1], heads)
        out = [
            x[:, j * HEAD_DIM : (j + 1) * HEAD_DIM] / x[:, cw + 64 + j : cw + 65 + j]
            for j in range(heads)
        ]
        cut = pl.ds(pl.multiple_of(c * cw, LANES), cw)
        o_ref[:, cut] = jnp.concatenate(out, axis=1).astype(jnp.bfloat16)

    def when(low, t, high, do, c):
        @pl.when(jnp.logical_and(t >= low, t < high))
        def _():
            do(c)

    def open_chunk(c):
        kv_copy(c, 0).wait()
        kv_copy(c, 1).wait()
        attend(c, 0, jnp.zeros((total, LANES), jnp.float32))

    def close_chunk(c):
        stats = part[c, :, :, cw:].reshape(total, LANES)
        for pair in range(1, heads // 2):
            stats = attend(c, pair, stats)
        a_copy(c).start()

    def step(t, _):
        when(1, t, chunks, gather_sibling, t)
        when(0, t, chunks, open_chunk, t)
        when(0, t, chunks - 2, gather_far, t + 2)
        when(0, t, chunks - 1, gather_across, t + 1)
        when(1, t, chunks + 1, merge_a, t - 1)
        when(2, t, chunks + 2, merge_b, t - 2)
        when(3, t, chunks + 3, finish, t - 3)
        when(0, t, chunks, close_chunk, t)
        return 0

    lax.fori_loop(0, chunks + 3, step, 0)

    for c in range(chunks):
        for number in range(2 * far - 1 + chips):
            gather_copy(c, my_slot, sibling, number).wait_send()
        a_copy(c).wait_send()
        b_copy(c).wait_send()
        for d in range(1, far):
            c_copy(c, d).wait_send()


def local(n, queries, cache_keys, cache_values, span_keys, span_values, cache_tokens, span_start):
    own, width = queries.shape
    rows = cache_keys.shape[0]
    heads = width // HEAD_DIM
    chunks = heads // (4 if heads % 4 == 0 else 2)
    chips = n // 2
    far = chips // 2
    total = n * own
    cs = width // chunks + LANES
    smem = pl.BlockSpec(memory_space=pltpu.SMEM)
    vmem = pl.BlockSpec(memory_space=pltpu.VMEM)
    hbm = pl.BlockSpec(memory_space=pl.ANY)
    dma = pltpu.SemaphoreType.DMA
    return pl.pallas_call(
        functools.partial(kernel, n, chunks),
        out_shape=jax.ShapeDtypeStruct((own, width), jnp.bfloat16),
        in_specs=[smem, smem, vmem, hbm, hbm, vmem, vmem],
        out_specs=vmem,
        scratch_shapes=[
            pltpu.VMEM((chunks, n, own, width // chunks), jnp.bfloat16),
            pltpu.VMEM((rows + LANES, width), jnp.bfloat16),
            pltpu.VMEM((rows + LANES, width), jnp.bfloat16),
            pltpu.VMEM((chunks, n, own, cs), jnp.float32),
            pltpu.VMEM((chunks, chips, own, cs), jnp.float32),
            pltpu.VMEM((chunks, far, own, cs), jnp.float32),
            pltpu.VMEM((chunks, far - 1, own, cs), jnp.float32),
            pltpu.VMEM((1, rows), jnp.float32),
            pltpu.VMEM((2 * total, LANES), jnp.float32),
            dma((2, chunks)),
            dma((chunks, far - 1 + far + chips)),
            dma((chunks, n)),
            dma((chunks,)),
            dma((chunks,)),
            dma((chunks,)),
            dma((chunks,)),
            dma((chunks, far - 1)),
            dma((chunks, far - 1)),
        ],
        compiler_params=pltpu.CompilerParams(
            collective_id=0, has_side_effects=True, vmem_limit_bytes=56 * 1024 * 1024
        ),
    )(cache_tokens, span_start, queries, cache_keys, cache_values, span_keys, span_values)


def solution(mesh):
    placed = (
        P(("groups", "seq"), None),
        P(("groups", "seq"), None),
        P(("groups", "seq"), None),
        P(("groups", "seq"), None),
        P(("groups", "seq"), None),
        P("groups"),
        P("groups"),
    )
    return jax.shard_map(
        functools.partial(local, mesh.shape["seq"]),
        mesh=mesh, in_specs=placed, out_specs=P(("groups", "seq"), None), check_vma=False,
    )
```

```python
import functools
import math

import jax
import jax.numpy as jnp
from jax import lax
from jax.experimental import pallas as pl
from jax.experimental.pallas import tpu as pltpu
from jax.sharding import PartitionSpec as P

HEAD_DIM = 128
FRAME_TOK = 1560
NEG_FILL = -1e30
LANES = 128
MESH = pl.DeviceIdType.MESH


def merge(x, y, heads):
    width = heads * HEAD_DIM
    sx, sy = x[:, width:], y[:, width:]
    top = jnp.maximum(sx, sy)
    fx, fy = jnp.exp2(sx - top), jnp.exp2(sy - top)
    lane = lax.broadcasted_iota(jnp.int32, sx.shape, 1)
    den = sx * pltpu.roll(fx, 64, 1) + sy * pltpu.roll(fy, 64, 1)
    pieces = []
    for j in range(heads):
        cut = slice(j * HEAD_DIM, (j + 1) * HEAD_DIM)
        pieces.append(x[:, cut] * fx[:, j : j + 1] + y[:, cut] * fy[:, j : j + 1])
    pieces.append(jnp.where(lane < 64, top, den))
    return jnp.concatenate(pieces, axis=1)


def kernel(
    n, chunks,
    tok_ref, start_ref, q_ref, k_hbm, v_hbm, sk_ref, sv_ref, o_ref,
    qg, kbuf, vbuf, part, ra, rb, rc, bias_row, bias_span,
    kv_sem, g_send, g_recv, a_send, a_recv, b_send, b_recv, c_send, c_recv,
):
    rows, width = k_hbm.shape
    own = q_ref.shape[0]
    chips = n // 2
    far = chips // 2
    total = n * own
    heads = width // HEAD_DIM // chunks
    cw = heads * HEAD_DIM
    cs = cw + LANES
    coef = math.log2(math.e) / math.sqrt(HEAD_DIM)

    me = lax.axis_index("seq")
    group = lax.axis_index("groups")
    core = lax.rem(me, 2)
    side = lax.rem(me // 2, 2)
    hi = me // 4

    def device(hi_, side_, core_):
        return (group, (hi_ * 2 + side_) * 2 + core_)

    def slot_of(hi_, side_, core_):
        return core_ * chips + side_ * far + hi_

    sibling = device(hi, side, 1 - core)
    across = device(hi, 1 - side, core)

    def kv_copy(c, which):
        cut = pl.ds(pl.multiple_of(c * cw, LANES), cw)
        src, dst = (k_hbm, kbuf) if which == 0 else (v_hbm, vbuf)
        return pltpu.make_async_copy(
            src.at[:, cut], dst.at[pl.ds(0, rows), cut], kv_sem.at[which, c]
        )

    for c in range(chunks):
        kv_copy(c, 0).start()
        kv_copy(c, 1).start()

    barrier = pltpu.get_barrier_semaphore()
    pl.semaphore_signal(barrier, inc=1, device_id=sibling, device_id_type=MESH)
    pl.semaphore_signal(barrier, inc=1, device_id=across, device_id_type=MESH)
    for d in range(1, far):
        pl.semaphore_signal(
            barrier, inc=1, device_id=device(lax.rem(hi + d, far), side, core), device_id_type=MESH
        )

    my_slot = slot_of(hi, side, core)
    qg[pl.ds(my_slot, 1)] = q_ref[...][None]

    pl.semaphore_wait(barrier, far + 1)

    def gather_copy(slot, to, number):
        return pltpu.make_async_remote_copy(
            src_ref=qg.at[slot], dst_ref=qg.at[slot],
            send_sem=g_send.at[number], recv_sem=g_recv.at[slot],
            device_id=to, device_id_type=MESH,
        )

    sends = []

    def gather_send(slot, to):
        copy = gather_copy(slot, to, len(sends))
        copy.start()
        sends.append(copy)

    def gather_wait(slot):
        gather_copy(slot, sibling, 0).wait_recv()

    for d in range(1, far):
        gather_send(my_slot, device(lax.rem(hi + d, far), side, core))
    gather_send(my_slot, across)
    gather_send(my_slot, sibling)

    position = me * rows + lax.broadcasted_iota(jnp.int32, bias_row.shape, 1)
    bias_row[...] = jnp.where(position < tok_ref[0], 0.0, NEG_FILL)
    shape = (total, LANES)
    row = lax.broadcasted_iota(jnp.int32, shape, 0)
    lane = lax.broadcasted_iota(jnp.int32, shape, 1)
    token = row
    for s in range(n):
        s_core, s_side, s_hi = s // chips, (s % chips) // far, s % far
        owner = (s_hi * 2 + s_side) * 2 + s_core
        inside = jnp.logical_and(row >= s * own, row < (s + 1) * own)
        token = jnp.where(inside, row + (owner - s) * own, token)
    key = me * own + lane
    seen = lane < own
    for f in range(1, (FRAME_TOK - 1 + total) // FRAME_TOK + 1):
        edge = f * FRAME_TOK - start_ref[0]
        seen = jnp.logical_and(seen, jnp.logical_or(key < edge, token >= edge))
    bias_span[...] = jnp.where(seen, 0.0, NEG_FILL)
    pad = jnp.zeros((LANES - own, width), jnp.float32)
    for ref, buf in ((sk_ref, kbuf), (sv_ref, vbuf)):
        block = jnp.concatenate([ref[...].astype(jnp.float32), pad], axis=0)
        buf[pl.ds(rows, LANES), :] = block.astype(jnp.bfloat16)

    for d in range(1, far):
        slot = slot_of(lax.rem(hi - d + far, far), side, core)
        gather_wait(slot)
        gather_send(slot, across)
        gather_send(slot, sibling)
    for d in range(far):
        slot = slot_of(lax.rem(hi - d + far, far), 1 - side, core)
        gather_wait(slot)
        gather_send(slot, sibling)
    for s_side in (side, 1 - side):
        for d in range(far):
            gather_wait(slot_of(lax.rem(hi - d + far, far), s_side, 1 - core))

    def a_copy(c):
        return pltpu.make_async_remote_copy(
            src_ref=part.at[c, pl.ds((1 - core) * chips, chips)], dst_ref=ra.at[c],
            send_sem=a_send.at[c], recv_sem=a_recv.at[c],
            device_id=sibling, device_id_type=MESH,
        )

    def b_copy(c):
        return pltpu.make_async_remote_copy(
            src_ref=part.at[c, pl.ds(core * chips + (1 - side) * far, far)], dst_ref=rb.at[c],
            send_sem=b_send.at[c], recv_sem=b_recv.at[c],
            device_id=across, device_id_type=MESH,
        )

    def c_copy(c, d):
        other = lax.rem(hi + d, far)
        return pltpu.make_async_remote_copy(
            src_ref=part.at[c, slot_of(other, side, core)], dst_ref=rc.at[c, d - 1],
            send_sem=c_send.at[c, d - 1], recv_sem=c_recv.at[c, d - 1],
            device_id=device(other, side, core), device_id_type=MESH,
        )

    def attend(c, first, last):
        stat_lane = lax.broadcasted_iota(jnp.int32, (total, LANES), 1)
        if first == 0:
            stats = jnp.zeros((total, LANES), jnp.float32)
        else:
            stats = part[c, :, :, cw:].reshape(total, LANES)
        for j in range(first, last):
            cut = pl.ds(pl.multiple_of(c * cw + j * HEAD_DIM, LANES), HEAD_DIM)
            q = qg[:, :, cut].astype(jnp.float32).reshape(total, HEAD_DIM).astype(jnp.bfloat16)
            s = lax.dot_general(
                q, kbuf[:, cut], (((1,), (1,)), ((), ())), preferred_element_type=jnp.float32
            ) * coef
            s_cache = s[:, :rows] + bias_row[...]
            s_span = s[:, rows:] + bias_span[...]
            s = jnp.concatenate([s_cache, s_span], axis=1)
            top = jnp.max(s, axis=1, keepdims=True)
            w = jnp.exp2(s - top)
            den = jnp.sum(w, axis=1, keepdims=True)
            num = jnp.dot(w.astype(jnp.bfloat16), vbuf[:, cut], preferred_element_type=jnp.float32)
            part[c, :, :, j * HEAD_DIM : (j + 1) * HEAD_DIM] = num.reshape(n, own, HEAD_DIM)
            stats = jnp.where(stat_lane == j, top, stats)
            stats = jnp.where(stat_lane == 64 + j, den, stats)
        part[c, :, :, cw:] = stats.reshape(n, own, LANES)

    def merge_a(c):
        a_copy(c).wait_recv()
        mine = pl.ds(core * chips, chips)
        x = part[c, mine].reshape(chips * own, cs)
        y = ra[c].reshape(chips * own, cs)
        part[c, mine] = merge(x, y, heads).reshape(chips, own, cs)
        b_copy(c).start()

    def merge_b(c):
        b_copy(c).wait_recv()
        mine = pl.ds(core * chips + side * far, far)
        x = part[c, mine].reshape(far * own, cs)
        y = rb[c].reshape(far * own, cs)
        part[c, mine] = merge(x, y, heads).reshape(far, own, cs)
        for d in range(1, far):
            c_copy(c, d).start()

    def finish(c):
        x = part[c, my_slot]
        for d in range(1, far):
            c_copy(c, d).wait_recv()
            x = merge(x, rc[c, d - 1], heads)
        out = [
            x[:, j * HEAD_DIM : (j + 1) * HEAD_DIM] / x[:, cw + 64 + j : cw + 65 + j]
            for j in range(heads)
        ]
        cut = pl.ds(pl.multiple_of(c * cw, LANES), cw)
        o_ref[:, cut] = jnp.concatenate(out, axis=1).astype(jnp.bfloat16)

    def when(low, t, high, do, c):
        @pl.when(jnp.logical_and(t >= low, t < high))
        def _():
            do(c)

    half = heads // 2

    def open_chunk(c):
        kv_copy(c, 0).wait()
        kv_copy(c, 1).wait()
        attend(c, 0, half)

    def close_chunk(c):
        attend(c, half, heads)
        a_copy(c).start()

    def step(t, _):
        when(0, t, chunks, open_chunk, t)
        when(1, t, chunks + 1, merge_a, t - 1)
        when(2, t, chunks + 2, merge_b, t - 2)
        when(3, t, chunks + 3, finish, t - 3)
        when(0, t, chunks, close_chunk, t)
        return 0

    lax.fori_loop(0, chunks + 3, step, 0)

    for copy in sends:
        copy.wait_send()
    for c in range(chunks):
        a_copy(c).wait_send()
        b_copy(c).wait_send()
        for d in range(1, far):
            c_copy(c, d).wait_send()


def local(n, queries, cache_keys, cache_values, span_keys, span_values, cache_tokens, span_start):
    own, width = queries.shape
    rows = cache_keys.shape[0]
    heads = width // HEAD_DIM
    chunks = 4 if heads % 4 == 0 else 1
    chips = n // 2
    far = chips // 2
    total = n * own
    cs = width // chunks + LANES
    smem = pl.BlockSpec(memory_space=pltpu.SMEM)
    vmem = pl.BlockSpec(memory_space=pltpu.VMEM)
    hbm = pl.BlockSpec(memory_space=pl.ANY)
    dma = pltpu.SemaphoreType.DMA
    return pl.pallas_call(
        functools.partial(kernel, n, chunks),
        out_shape=jax.ShapeDtypeStruct((own, width), jnp.bfloat16),
        in_specs=[smem, smem, vmem, hbm, hbm, vmem, vmem],
        out_specs=vmem,
        scratch_shapes=[
            pltpu.VMEM((n, own, width), jnp.bfloat16),
            pltpu.VMEM((rows + LANES, width), jnp.bfloat16),
            pltpu.VMEM((rows + LANES, width), jnp.bfloat16),
            pltpu.VMEM((chunks, n, own, cs), jnp.float32),
            pltpu.VMEM((chunks, chips, own, cs), jnp.float32),
            pltpu.VMEM((chunks, far, own, cs), jnp.float32),
            pltpu.VMEM((chunks, far - 1, own, cs), jnp.float32),
            pltpu.VMEM((1, rows), jnp.float32),
            pltpu.VMEM((total, LANES), jnp.float32),
            dma((2, chunks)),
            dma((far - 1 + far + chips,)),
            dma((n,)),
            dma((chunks,)),
            dma((chunks,)),
            dma((chunks,)),
            dma((chunks,)),
            dma((chunks, far - 1)),
            dma((chunks, far - 1)),
        ],
        compiler_params=pltpu.CompilerParams(
            collective_id=0, has_side_effects=True, vmem_limit_bytes=56 * 1024 * 1024
        ),
    )(cache_tokens, span_start, queries, cache_keys, cache_values, span_keys, span_values)


def solution(mesh):
    placed = (
        P(("groups", "seq"), None),
        P(("groups", "seq"), None),
        P(("groups", "seq"), None),
        P(("groups", "seq"), None),
        P(("groups", "seq"), None),
        P("groups"),
        P("groups"),
    )
    return jax.shard_map(
        functools.partial(local, mesh.shape["seq"]),
        mesh=mesh, in_specs=placed, out_specs=P(("groups", "seq"), None), check_vma=False,
    )
```

```python
import functools
import math

import jax
import jax.numpy as jnp
from jax import lax
from jax.experimental import pallas as pl
from jax.experimental.pallas import tpu as pltpu
from jax.sharding import PartitionSpec as P

HEAD_DIM = 128
FRAME_TOK = 1560
NEG_FILL = -(2.0**100)
SPREAD = 240.0
LANES = 128
MESH = pl.DeviceIdType.MESH


def two_parts(x):
    high = x.astype(jnp.bfloat16).astype(jnp.float32)
    return high, (x - high).astype(jnp.bfloat16).astype(jnp.float32)


def code(x, heads):
    width = heads * HEAD_DIM
    stats = x[:, width:]
    high, low = two_parts(stats)
    tile = high + pltpu.roll(low, 16, 1)
    lane = lax.broadcasted_iota(jnp.int32, stats.shape, 1)
    pieces = []
    for j in range(heads):
        v = x[:, j * HEAD_DIM : (j + 1) * HEAD_DIM]
        size = jnp.abs(v)
        largest = jnp.max(size, axis=1, keepdims=True)
        largest = largest.astype(jnp.bfloat16).astype(jnp.float32)
        y = jnp.exp2(size * (SPREAD / jnp.maximum(largest, 1e-30)) - SPREAD / 2)
        pieces.append(jnp.where(v < 0.0, -y, y).astype(jnp.bfloat16))
        tile = jnp.where(lane == 32 + j, largest, tile)
    pieces.append(tile.astype(jnp.bfloat16))
    return jnp.concatenate(pieces, axis=1)


def decode(y, heads):
    width = heads * HEAD_DIM
    tile = y[:, width:].astype(jnp.float32)
    lane = lax.broadcasted_iota(jnp.int32, tile.shape, 1)
    kept = jnp.logical_or(lane < 16, jnp.logical_and(lane >= 64, lane < 80))
    stats = jnp.where(kept, tile + pltpu.roll(tile, LANES - 16, 1), 0.0)
    pieces = []
    for j in range(heads):
        v = y[:, j * HEAD_DIM : (j + 1) * HEAD_DIM].astype(jnp.float32)
        size = jnp.log(jnp.abs(v)) * (1.0 / (SPREAD * math.log(2.0))) + 0.5
        size = size * tile[:, 32 + j : 33 + j]
        pieces.append(jnp.where(v < 0.0, -size, size))
    pieces.append(stats)
    return jnp.concatenate(pieces, axis=1)


def merge(x, y, heads):
    width = heads * HEAD_DIM
    sx, sy = x[:, width:], y[:, width:]
    top = jnp.maximum(sx, sy)
    fx, fy = jnp.exp2(sx - top), jnp.exp2(sy - top)
    lane = lax.broadcasted_iota(jnp.int32, sx.shape, 1)
    den = sx * pltpu.roll(fx, 64, 1) + sy * pltpu.roll(fy, 64, 1)
    pieces = []
    for j in range(heads):
        cut = slice(j * HEAD_DIM, (j + 1) * HEAD_DIM)
        pieces.append(x[:, cut] * fx[:, j : j + 1] + y[:, cut] * fy[:, j : j + 1])
    pieces.append(jnp.where(lane < 64, top, den))
    return jnp.concatenate(pieces, axis=1)


def kernel(
    n, chunks,
    tok_ref, start_ref, q_ref, k_hbm, v_hbm, sk_ref, sv_ref, o_ref,
    qg, kbuf, vbuf, part, ea, eb, ec, ra, rb, rc, bias_row, bias_span,
    kv_sem, g_send, g_recv, a_send, a_recv, b_send, b_recv, c_send, c_recv,
):
    rows, width = k_hbm.shape
    own = q_ref.shape[0]
    chips = n // 2
    far = chips // 2
    total = n * own
    heads = width // HEAD_DIM // chunks
    cw = heads * HEAD_DIM
    cs = cw + LANES
    coef = math.log2(math.e) / math.sqrt(HEAD_DIM)

    me = lax.axis_index("seq")
    group = lax.axis_index("groups")
    core = lax.rem(me, 2)
    side = lax.rem(me // 2, 2)
    hi = me // 4

    def device(hi_, side_, core_):
        return (group, (hi_ * 2 + side_) * 2 + core_)

    def slot_of(hi_, side_, core_):
        return core_ * chips + side_ * far + hi_

    sibling = device(hi, side, 1 - core)
    across = device(hi, 1 - side, core)

    def kv_copy(c, which):
        cut = pl.ds(pl.multiple_of(c * cw, LANES), cw)
        src, dst = (k_hbm, kbuf) if which == 0 else (v_hbm, vbuf)
        return pltpu.make_async_copy(
            src.at[:, cut], dst.at[pl.ds(0, rows), cut], kv_sem.at[which, c]
        )

    for c in range(chunks):
        kv_copy(c, 0).start()
        kv_copy(c, 1).start()

    barrier = pltpu.get_barrier_semaphore()
    pl.semaphore_signal(barrier, inc=1, device_id=sibling, device_id_type=MESH)
    pl.semaphore_signal(barrier, inc=1, device_id=across, device_id_type=MESH)
    for d in range(1, far):
        pl.semaphore_signal(
            barrier, inc=1, device_id=device(lax.rem(hi + d, far), side, core), device_id_type=MESH
        )

    my_slot = slot_of(hi, side, core)
    qg[pl.ds(my_slot, 1)] = q_ref[...][None]

    pl.semaphore_wait(barrier, far + 1)

    def gather_copy(slot, to, number):
        return pltpu.make_async_remote_copy(
            src_ref=qg.at[slot], dst_ref=qg.at[slot],
            send_sem=g_send.at[number], recv_sem=g_recv.at[slot],
            device_id=to, device_id_type=MESH,
        )

    sends = []

    def gather_send(slot, to):
        copy = gather_copy(slot, to, len(sends))
        copy.start()
        sends.append(copy)

    def gather_wait(slot):
        gather_copy(slot, sibling, 0).wait_recv()

    for d in range(1, far):
        gather_send(my_slot, device(lax.rem(hi + d, far), side, core))
    gather_send(my_slot, across)
    gather_send(my_slot, sibling)

    position = me * rows + lax.broadcasted_iota(jnp.int32, bias_row.shape, 1)
    bias_row[...] = jnp.where(position < tok_ref[0], 0.0, NEG_FILL)
    shape = (total, LANES)
    row = lax.broadcasted_iota(jnp.int32, shape, 0)
    lane = lax.broadcasted_iota(jnp.int32, shape, 1)
    token = row
    for s in range(n):
        s_core, s_side, s_hi = s // chips, (s % chips) // far, s % far
        owner = (s_hi * 2 + s_side) * 2 + s_core
        inside = jnp.logical_and(row >= s * own, row < (s + 1) * own)
        token = jnp.where(inside, row + (owner - s) * own, token)
    key = me * own + lane
    seen = lane < own
    for f in range(1, (FRAME_TOK - 1 + total) // FRAME_TOK + 1):
        edge = f * FRAME_TOK - start_ref[0]
        seen = jnp.logical_and(seen, jnp.logical_or(key < edge, token >= edge))
    bias_span[...] = jnp.where(seen, 0.0, NEG_FILL)
    pad = jnp.zeros((LANES - own, width), jnp.float32)
    for ref, buf in ((sk_ref, kbuf), (sv_ref, vbuf)):
        block = jnp.concatenate([ref[...].astype(jnp.float32), pad], axis=0)
        buf[pl.ds(rows, LANES), :] = block.astype(jnp.bfloat16)

    for d in range(1, far):
        slot = slot_of(lax.rem(hi - d + far, far), side, core)
        gather_wait(slot)
        gather_send(slot, across)
        gather_send(slot, sibling)
    for d in range(far):
        slot = slot_of(lax.rem(hi - d + far, far), 1 - side, core)
        gather_wait(slot)
        gather_send(slot, sibling)
    for s_side in (side, 1 - side):
        for d in range(far):
            gather_wait(slot_of(lax.rem(hi - d + far, far), s_side, 1 - core))

    def a_copy(c):
        return pltpu.make_async_remote_copy(
            src_ref=ea.at[c], dst_ref=ra.at[c],
            send_sem=a_send.at[c], recv_sem=a_recv.at[c],
            device_id=sibling, device_id_type=MESH,
        )

    def b_copy(c):
        return pltpu.make_async_remote_copy(
            src_ref=eb.at[c], dst_ref=rb.at[c],
            send_sem=b_send.at[c], recv_sem=b_recv.at[c],
            device_id=across, device_id_type=MESH,
        )

    def c_copy(c, d):
        other = lax.rem(hi + d, far)
        return pltpu.make_async_remote_copy(
            src_ref=ec.at[c, d - 1], dst_ref=rc.at[c, d - 1],
            send_sem=c_send.at[c, d - 1], recv_sem=c_recv.at[c, d - 1],
            device_id=device(other, side, core), device_id_type=MESH,
        )

    def attend(c, first, last):
        stat_lane = lax.broadcasted_iota(jnp.int32, (total, LANES), 1)
        if first == 0:
            stats = jnp.zeros((total, LANES), jnp.float32)
        else:
            stats = part[c, :, :, cw:].reshape(total, LANES)
        for j in range(first, last):
            cut = pl.ds(pl.multiple_of(c * cw + j * HEAD_DIM, LANES), HEAD_DIM)
            q = qg[:, :, cut].astype(jnp.float32).reshape(total, HEAD_DIM).astype(jnp.bfloat16)
            s = lax.dot_general(
                q, kbuf[:, cut], (((1,), (1,)), ((), ())), preferred_element_type=jnp.float32
            ) * coef
            s_cache = s[:, :rows] + bias_row[...]
            s_span = s[:, rows:] + bias_span[...]
            s = jnp.concatenate([s_cache, s_span], axis=1)
            high, low = two_parts(jnp.max(s, axis=1, keepdims=True))
            top = high + low
            w = jnp.exp2(s - top)
            den = jnp.sum(w, axis=1, keepdims=True)
            num = jnp.dot(w.astype(jnp.bfloat16), vbuf[:, cut], preferred_element_type=jnp.float32)
            part[c, :, :, j * HEAD_DIM : (j + 1) * HEAD_DIM] = num.reshape(n, own, HEAD_DIM)
            stats = jnp.where(stat_lane == j, top, stats)
            stats = jnp.where(stat_lane == 64 + j, den, stats)
        part[c, :, :, cw:] = stats.reshape(n, own, LANES)

    def merge_a(c):
        a_copy(c).wait_recv()
        mine = pl.ds(core * chips, chips)
        x = part[c, mine].reshape(chips * own, cs)
        x = merge(x, decode(ra[c], heads), heads)
        part[c, mine] = x.reshape(chips, own, cs)
        theirs = part[c, pl.ds(core * chips + (1 - side) * far, far)]
        eb[c] = code(theirs.reshape(far * own, cs), heads)
        b_copy(c).start()

    def merge_b(c):
        b_copy(c).wait_recv()
        mine = pl.ds(core * chips + side * far, far)
        x = part[c, mine].reshape(far * own, cs)
        x = merge(x, decode(rb[c], heads), heads)
        part[c, mine] = x.reshape(far, own, cs)
        for d in range(1, far):
            ec[c, d - 1] = code(part[c, slot_of(lax.rem(hi + d, far), side, core)], heads)
            c_copy(c, d).start()

    def finish(c):
        x = part[c, my_slot]
        for d in range(1, far):
            c_copy(c, d).wait_recv()
            x = merge(x, decode(rc[c, d - 1], heads), heads)
        out = [
            x[:, j * HEAD_DIM : (j + 1) * HEAD_DIM] / x[:, cw + 64 + j : cw + 65 + j]
            for j in range(heads)
        ]
        cut = pl.ds(pl.multiple_of(c * cw, LANES), cw)
        o_ref[:, cut] = jnp.concatenate(out, axis=1).astype(jnp.bfloat16)

    def when(low, t, high, do, c):
        @pl.when(jnp.logical_and(t >= low, t < high))
        def _():
            do(c)

    half = heads // 2

    def open_chunk(c):
        kv_copy(c, 0).wait()
        kv_copy(c, 1).wait()
        attend(c, 0, half)

    def close_chunk(c):
        attend(c, half, heads)
        theirs = part[c, pl.ds((1 - core) * chips, chips)]
        ea[c] = code(theirs.reshape(chips * own, cs), heads)
        a_copy(c).start()

    def step(t, _):
        when(0, t, chunks, open_chunk, t)
        when(1, t, chunks + 1, merge_a, t - 1)
        when(2, t, chunks + 2, merge_b, t - 2)
        when(3, t, chunks + 3, finish, t - 3)
        when(0, t, chunks, close_chunk, t)
        return 0

    lax.fori_loop(0, chunks + 3, step, 0)

    for copy in sends:
        copy.wait_send()
    for c in range(chunks):
        a_copy(c).wait_send()
        b_copy(c).wait_send()
        for d in range(1, far):
            c_copy(c, d).wait_send()


def local(n, queries, cache_keys, cache_values, span_keys, span_values, cache_tokens, span_start):
    own, width = queries.shape
    rows = cache_keys.shape[0]
    heads = width // HEAD_DIM
    chunks = 4 if heads % 4 == 0 else 1
    chips = n // 2
    far = chips // 2
    total = n * own
    cs = width // chunks + LANES
    smem = pl.BlockSpec(memory_space=pltpu.SMEM)
    vmem = pl.BlockSpec(memory_space=pltpu.VMEM)
    hbm = pl.BlockSpec(memory_space=pl.ANY)
    dma = pltpu.SemaphoreType.DMA
    return pl.pallas_call(
        functools.partial(kernel, n, chunks),
        out_shape=jax.ShapeDtypeStruct((own, width), jnp.bfloat16),
        in_specs=[smem, smem, vmem, hbm, hbm, vmem, vmem],
        out_specs=vmem,
        scratch_shapes=[
            pltpu.VMEM((n, own, width), jnp.bfloat16),
            pltpu.VMEM((rows + LANES, width), jnp.bfloat16),
            pltpu.VMEM((rows + LANES, width), jnp.bfloat16),
            pltpu.VMEM((chunks, n, own, cs), jnp.float32),
            pltpu.VMEM((chunks, chips * own, cs), jnp.bfloat16),
            pltpu.VMEM((chunks, far * own, cs), jnp.bfloat16),
            pltpu.VMEM((chunks, far - 1, own, cs), jnp.bfloat16),
            pltpu.VMEM((chunks, chips * own, cs), jnp.bfloat16),
            pltpu.VMEM((chunks, far * own, cs), jnp.bfloat16),
            pltpu.VMEM((chunks, far - 1, own, cs), jnp.bfloat16),
            pltpu.VMEM((1, rows), jnp.float32),
            pltpu.VMEM((total, LANES), jnp.float32),
            dma((2, chunks)),
            dma((far - 1 + far + chips,)),
            dma((n,)),
            dma((chunks,)),
            dma((chunks,)),
            dma((chunks,)),
            dma((chunks,)),
            dma((chunks, far - 1)),
            dma((chunks, far - 1)),
        ],
        compiler_params=pltpu.CompilerParams(
            collective_id=0, has_side_effects=True, vmem_limit_bytes=56 * 1024 * 1024
        ),
    )(cache_tokens, span_start, queries, cache_keys, cache_values, span_keys, span_values)


def solution(mesh):
    placed = (
        P(("groups", "seq"), None),
        P(("groups", "seq"), None),
        P(("groups", "seq"), None),
        P(("groups", "seq"), None),
        P(("groups", "seq"), None),
        P("groups"),
        P("groups"),
    )
    return jax.shard_map(
        functools.partial(local, mesh.shape["seq"]),
        mesh=mesh, in_specs=placed, out_specs=P(("groups", "seq"), None), check_vma=False,
    )
```

```python
import functools
import math

import jax
import jax.numpy as jnp
from jax import lax
from jax.experimental import pallas as pl
from jax.experimental.pallas import tpu as pltpu
from jax.sharding import PartitionSpec as P

HEAD_DIM = 128
FRAME_TOK = 1560
NEG_FILL = -(2.0**100)
SPREAD = 240.0
LANES = 128
MESH = pl.DeviceIdType.MESH


def two_parts(x):
    high = x.astype(jnp.bfloat16).astype(jnp.float32)
    return high, (x - high).astype(jnp.bfloat16).astype(jnp.float32)


def code(x, heads):
    width = heads * HEAD_DIM
    stats = x[:, width:]
    high, low = two_parts(stats)
    tile = high + pltpu.roll(low, 16, 1)
    lane = lax.broadcasted_iota(jnp.int32, stats.shape, 1)
    pieces = []
    for j in range(heads):
        v = x[:, j * HEAD_DIM : (j + 1) * HEAD_DIM]
        size = jnp.abs(v)
        largest = jnp.max(size, axis=1, keepdims=True)
        largest = largest.astype(jnp.bfloat16).astype(jnp.float32)
        y = jnp.exp2(size * (SPREAD / jnp.maximum(largest, 1e-30)) - SPREAD / 2)
        pieces.append(jnp.where(v < 0.0, -y, y).astype(jnp.bfloat16))
        tile = jnp.where(lane == 32 + j, largest, tile)
    pieces.append(tile.astype(jnp.bfloat16))
    return jnp.concatenate(pieces, axis=1)


def decode(y, heads):
    width = heads * HEAD_DIM
    tile = y[:, width:].astype(jnp.float32)
    lane = lax.broadcasted_iota(jnp.int32, tile.shape, 1)
    kept = jnp.logical_or(lane < 16, jnp.logical_and(lane >= 64, lane < 80))
    stats = jnp.where(kept, tile + pltpu.roll(tile, LANES - 16, 1), 0.0)
    pieces = []
    for j in range(heads):
        v = y[:, j * HEAD_DIM : (j + 1) * HEAD_DIM].astype(jnp.float32)
        size = jnp.log(jnp.abs(v)) * (1.0 / (SPREAD * math.log(2.0))) + 0.5
        size = size * tile[:, 32 + j : 33 + j]
        pieces.append(jnp.where(v < 0.0, -size, size))
    pieces.append(stats)
    return jnp.concatenate(pieces, axis=1)


def merge(x, y, heads):
    width = heads * HEAD_DIM
    sx, sy = x[:, width:], y[:, width:]
    top = jnp.maximum(sx, sy)
    fx, fy = jnp.exp2(sx - top), jnp.exp2(sy - top)
    lane = lax.broadcasted_iota(jnp.int32, sx.shape, 1)
    den = sx * pltpu.roll(fx, 64, 1) + sy * pltpu.roll(fy, 64, 1)
    pieces = []
    for j in range(heads):
        cut = slice(j * HEAD_DIM, (j + 1) * HEAD_DIM)
        pieces.append(x[:, cut] * fx[:, j : j + 1] + y[:, cut] * fy[:, j : j + 1])
    pieces.append(jnp.where(lane < 64, top, den))
    return jnp.concatenate(pieces, axis=1)


def gather_kernel(n, q_ref, qg, g_send, g_recv):
    chips = n // 2
    far = chips // 2
    me = lax.axis_index("seq")
    group = lax.axis_index("groups")
    core = lax.rem(me, 2)
    side = lax.rem(me // 2, 2)
    hi = me // 4

    def device(hi_, side_, core_):
        return (group, (hi_ * 2 + side_) * 2 + core_)

    def slot_of(hi_, side_, core_):
        return core_ * chips + side_ * far + hi_

    sibling = device(hi, side, 1 - core)
    across = device(hi, 1 - side, core)

    barrier = pltpu.get_barrier_semaphore()
    pl.semaphore_signal(barrier, inc=1, device_id=sibling, device_id_type=MESH)
    pl.semaphore_signal(barrier, inc=1, device_id=across, device_id_type=MESH)
    for d in range(1, far):
        pl.semaphore_signal(
            barrier, inc=1, device_id=device(lax.rem(hi + d, far), side, core), device_id_type=MESH
        )
    my_slot = slot_of(hi, side, core)
    qg[pl.ds(my_slot, 1)] = q_ref[...][None]

    pl.semaphore_wait(barrier, far + 1)

    def gather_copy(slot, to, number):
        return pltpu.make_async_remote_copy(
            src_ref=qg.at[slot], dst_ref=qg.at[slot],
            send_sem=g_send.at[number], recv_sem=g_recv.at[slot],
            device_id=to, device_id_type=MESH,
        )

    sends = []

    def gather_send(slot, to):
        copy = gather_copy(slot, to, len(sends))
        copy.start()
        sends.append(copy)

    def gather_wait(slot):
        gather_copy(slot, sibling, 0).wait_recv()

    for d in range(1, far):
        gather_send(my_slot, device(lax.rem(hi + d, far), side, core))
    gather_send(my_slot, across)
    gather_send(my_slot, sibling)

    for d in range(1, far):
        slot = slot_of(lax.rem(hi - d + far, far), side, core)
        gather_wait(slot)
        gather_send(slot, across)
        gather_send(slot, sibling)
    for d in range(far):
        slot = slot_of(lax.rem(hi - d + far, far), 1 - side, core)
        gather_wait(slot)
        gather_send(slot, sibling)
    for s_side in (side, 1 - side):
        for d in range(far):
            gather_wait(slot_of(lax.rem(hi - d + far, far), s_side, 1 - core))
    for copy in sends:
        copy.wait_send()


def attend_kernel(n, heads, tok_ref, start_ref, q_ref, k_ref, v_ref, sk_ref, sv_ref, part, skp, svp):
    rows = k_ref.shape[0]
    own = sk_ref.shape[0]
    chips = n // 2
    far = chips // 2
    total = n * own
    cw = heads * HEAD_DIM
    coef = math.log2(math.e) / math.sqrt(HEAD_DIM)
    me = lax.axis_index("seq")
    position = me * rows + lax.broadcasted_iota(jnp.int32, (1, rows), 1)
    bias_row = jnp.where(position < tok_ref[0], 0.0, NEG_FILL)
    shape = (total, LANES)
    row = lax.broadcasted_iota(jnp.int32, shape, 0)
    lane = lax.broadcasted_iota(jnp.int32, shape, 1)
    token = row
    for s in range(n):
        s_core, s_side, s_hi = s // chips, (s % chips) // far, s % far
        owner = (s_hi * 2 + s_side) * 2 + s_core
        inside = jnp.logical_and(row >= s * own, row < (s + 1) * own)
        token = jnp.where(inside, row + (owner - s) * own, token)
    key = me * own + lane
    seen = lane < own
    for f in range(1, (FRAME_TOK - 1 + total) // FRAME_TOK + 1):
        edge = f * FRAME_TOK - start_ref[0]
        seen = jnp.logical_and(seen, jnp.logical_or(key < edge, token >= edge))
    bias_span = jnp.where(seen, 0.0, NEG_FILL)
    pad = jnp.zeros((LANES - own, cw), jnp.float32)
    for ref, buf in ((sk_ref, skp), (sv_ref, svp)):
        block = jnp.concatenate([ref[...].astype(jnp.float32), pad], axis=0)
        buf[...] = block.astype(jnp.bfloat16)

    def scores(j):
        cut = slice(j * HEAD_DIM, (j + 1) * HEAD_DIM)
        q = q_ref[:, :, cut].astype(jnp.float32).reshape(total, HEAD_DIM).astype(jnp.bfloat16)
        nt = (((1,), (1,)), ((), ()))
        s_cache = lax.dot_general(q, k_ref[:, cut], nt, preferred_element_type=jnp.float32)
        s_span = lax.dot_general(q, skp[:, cut], nt, preferred_element_type=jnp.float32)
        return s_cache * coef + bias_row, s_span * coef + bias_span

    stats = jnp.zeros(shape, jnp.float32)
    ahead = scores(0)
    for j in range(heads):
        s_cache, s_span = ahead
        if j + 1 < heads:
            ahead = scores(j + 1)
        cut = slice(j * HEAD_DIM, (j + 1) * HEAD_DIM)
        top = jnp.maximum(
            jnp.max(s_cache, axis=1, keepdims=True), jnp.max(s_span, axis=1, keepdims=True)
        )
        high, low = two_parts(top)
        top = high + low
        w_cache, w_span = jnp.exp2(s_cache - top), jnp.exp2(s_span - top)
        den = jnp.sum(w_cache, axis=1, keepdims=True) + jnp.sum(w_span, axis=1, keepdims=True)
        num = jnp.dot(
            w_cache.astype(jnp.bfloat16), v_ref[:, cut], preferred_element_type=jnp.float32
        ) + jnp.dot(w_span.astype(jnp.bfloat16), svp[:, cut], preferred_element_type=jnp.float32)
        part[0, :, :, cut] = num.reshape(n, own, HEAD_DIM)
        stats = jnp.where(lane == j, top, stats)
        stats = jnp.where(lane == 64 + j, den, stats)
    part[0, :, :, cw:] = stats.reshape(n, own, LANES)


def reduce_kernel(
    n, part_ref, o_ref, part, ea, eb, ec, ra, rb, rc,
    a_send, a_recv, b_send, b_recv, c_send, c_recv,
):
    chunks, _, own, cs = part_ref.shape
    cw = cs - LANES
    heads = cw // HEAD_DIM
    chips = n // 2
    far = chips // 2
    me = lax.axis_index("seq")
    group = lax.axis_index("groups")
    core = lax.rem(me, 2)
    side = lax.rem(me // 2, 2)
    hi = me // 4

    def device(hi_, side_, core_):
        return (group, (hi_ * 2 + side_) * 2 + core_)

    def slot_of(hi_, side_, core_):
        return core_ * chips + side_ * far + hi_

    sibling = device(hi, side, 1 - core)
    across = device(hi, 1 - side, core)

    barrier = pltpu.get_barrier_semaphore()
    pl.semaphore_signal(barrier, inc=1, device_id=sibling, device_id_type=MESH)
    pl.semaphore_signal(barrier, inc=1, device_id=across, device_id_type=MESH)
    for d in range(1, far):
        pl.semaphore_signal(
            barrier, inc=1, device_id=device(lax.rem(hi + d, far), side, core), device_id_type=MESH
        )

    my_slot = slot_of(hi, side, core)
    for c in range(chunks):
        theirs = part_ref[c, pl.ds((1 - core) * chips, chips)]
        ea[c] = code(theirs.reshape(chips * own, cs), heads)
    pl.semaphore_wait(barrier, far + 1)

    def a_copy(c):
        return pltpu.make_async_remote_copy(
            src_ref=ea.at[c], dst_ref=ra.at[c],
            send_sem=a_send.at[c], recv_sem=a_recv.at[c],
            device_id=sibling, device_id_type=MESH,
        )

    def b_copy(c):
        return pltpu.make_async_remote_copy(
            src_ref=eb.at[c], dst_ref=rb.at[c],
            send_sem=b_send.at[c], recv_sem=b_recv.at[c],
            device_id=across, device_id_type=MESH,
        )

    def c_copy(c, d):
        other = lax.rem(hi + d, far)
        return pltpu.make_async_remote_copy(
            src_ref=ec.at[c, d - 1], dst_ref=rc.at[c, d - 1],
            send_sem=c_send.at[c, d - 1], recv_sem=c_recv.at[c, d - 1],
            device_id=device(other, side, core), device_id_type=MESH,
        )

    def merge_a(c):
        a_copy(c).wait_recv()
        mine = pl.ds(core * chips, chips)
        x = part_ref[c, mine].reshape(chips * own, cs)
        x = merge(x, decode(ra[c], heads), heads)
        part[c, mine] = x.reshape(chips, own, cs)
        theirs = part[c, pl.ds(core * chips + (1 - side) * far, far)]
        eb[c] = code(theirs.reshape(far * own, cs), heads)
        b_copy(c).start()

    def merge_b(c):
        b_copy(c).wait_recv()
        mine = pl.ds(core * chips + side * far, far)
        x = part[c, mine].reshape(far * own, cs)
        x = merge(x, decode(rb[c], heads), heads)
        part[c, mine] = x.reshape(far, own, cs)
        for d in range(1, far):
            ec[c, d - 1] = code(part[c, slot_of(lax.rem(hi + d, far), side, core)], heads)
            c_copy(c, d).start()

    def finish(c):
        x = part[c, my_slot]
        for d in range(1, far):
            c_copy(c, d).wait_recv()
            x = merge(x, decode(rc[c, d - 1], heads), heads)
        out = [
            x[:, j * HEAD_DIM : (j + 1) * HEAD_DIM] / x[:, cw + 64 + j : cw + 65 + j]
            for j in range(heads)
        ]
        cut = pl.ds(pl.multiple_of(c * cw, LANES), cw)
        o_ref[:, cut] = jnp.concatenate(out, axis=1).astype(jnp.bfloat16)

    for c in range(chunks):
        a_copy(c).start()

    def when(low, t, high, do, c):
        @pl.when(jnp.logical_and(t >= low, t < high))
        def _():
            do(c)

    def step(t, _):
        when(0, t, chunks, merge_a, t)
        when(1, t, chunks + 1, merge_b, t - 1)
        when(2, t, chunks + 2, finish, t - 2)
        return 0

    lax.fori_loop(0, chunks + 2, step, 0)
    for c in range(chunks):
        a_copy(c).wait_send()
        b_copy(c).wait_send()
        for d in range(1, far):
            c_copy(c, d).wait_send()


def local(n, queries, cache_keys, cache_values, span_keys, span_values, cache_tokens, span_start):
    own, width = queries.shape
    rows = cache_keys.shape[0]
    heads = width // HEAD_DIM
    chunks = 4 if heads % 4 == 0 else 1
    chips = n // 2
    far = chips // 2
    cw = width // chunks
    cs = cw + LANES
    smem = pl.BlockSpec(memory_space=pltpu.SMEM)
    vmem = pl.BlockSpec(memory_space=pltpu.VMEM)
    dma = pltpu.SemaphoreType.DMA
    limit = 56 * 1024 * 1024
    gathered = pl.pallas_call(
        functools.partial(gather_kernel, n),
        out_shape=jax.ShapeDtypeStruct((n, own, width), jnp.bfloat16),
        in_specs=[vmem],
        out_specs=vmem,
        scratch_shapes=[dma((far - 1 + far + chips,)), dma((n,))],
        compiler_params=pltpu.CompilerParams(
            collective_id=0, has_side_effects=True, vmem_limit_bytes=limit
        ),
    )(queries)
    part = pl.pallas_call(
        functools.partial(attend_kernel, n, heads // chunks),
        grid=(chunks,),
        out_shape=jax.ShapeDtypeStruct((chunks, n, own, cs), jnp.float32),
        in_specs=[
            smem, smem,
            pl.BlockSpec((n, own, cw), lambda i: (0, 0, i)),
            pl.BlockSpec((rows, cw), lambda i: (0, i)),
            pl.BlockSpec((rows, cw), lambda i: (0, i)),
            pl.BlockSpec((own, cw), lambda i: (0, i)),
            pl.BlockSpec((own, cw), lambda i: (0, i)),
        ],
        out_specs=pl.BlockSpec((1, n, own, cs), lambda i: (i, 0, 0, 0)),
        scratch_shapes=[pltpu.VMEM((LANES, cw), jnp.bfloat16)] * 2,
        compiler_params=pltpu.CompilerParams(vmem_limit_bytes=limit),
    )(cache_tokens, span_start, gathered, cache_keys, cache_values, span_keys, span_values)
    coded = [
        pltpu.VMEM((chunks, chips * own, cs), jnp.bfloat16),
        pltpu.VMEM((chunks, far * own, cs), jnp.bfloat16),
        pltpu.VMEM((chunks, far - 1, own, cs), jnp.bfloat16),
    ]
    return pl.pallas_call(
        functools.partial(reduce_kernel, n),
        out_shape=jax.ShapeDtypeStruct((own, width), jnp.bfloat16),
        in_specs=[vmem],
        out_specs=vmem,
        scratch_shapes=[pltpu.VMEM((chunks, n, own, cs), jnp.float32)] + coded * 2
        + [dma((chunks,))] * 4 + [dma((chunks, far - 1))] * 2,
        compiler_params=pltpu.CompilerParams(
            collective_id=1, has_side_effects=True, vmem_limit_bytes=limit
        ),
    )(part)


def solution(mesh):
    placed = (
        P(("groups", "seq"), None),
        P(("groups", "seq"), None),
        P(("groups", "seq"), None),
        P(("groups", "seq"), None),
        P(("groups", "seq"), None),
        P("groups"),
        P("groups"),
    )
    return jax.shard_map(
        functools.partial(local, mesh.shape["seq"]),
        mesh=mesh, in_specs=placed, out_specs=P(("groups", "seq"), None), check_vma=False,
    )
```

```python
import functools
import math

import jax
import jax.numpy as jnp
from jax import lax
from jax.experimental import pallas as pl
from jax.experimental.pallas import tpu as pltpu
from jax.sharding import PartitionSpec as P

HEAD_DIM = 128
FRAME_TOK = 1560
NEG_FILL = -(2.0**100)
SPREAD = 240.0
LANES = 128
MESH = pl.DeviceIdType.MESH


def two_parts(x):
    high = x.astype(jnp.bfloat16).astype(jnp.float32)
    return high, (x - high).astype(jnp.bfloat16).astype(jnp.float32)


def code(x, heads):
    width = heads * HEAD_DIM
    stats = x[:, width:]
    high, low = two_parts(stats)
    tile = high + pltpu.roll(low, 16, 1)
    lane = lax.broadcasted_iota(jnp.int32, stats.shape, 1)
    pieces = []
    for j in range(heads):
        v = x[:, j * HEAD_DIM : (j + 1) * HEAD_DIM]
        size = jnp.abs(v)
        largest = jnp.max(size, axis=1, keepdims=True)
        largest = largest.astype(jnp.bfloat16).astype(jnp.float32)
        y = jnp.exp2(size * (SPREAD / jnp.maximum(largest, 1e-30)) - SPREAD / 2)
        pieces.append(jnp.where(v < 0.0, -y, y).astype(jnp.bfloat16))
        tile = jnp.where(lane == 32 + j, largest, tile)
    pieces.append(tile.astype(jnp.bfloat16))
    return jnp.concatenate(pieces, axis=1)


def decode(y, heads):
    width = heads * HEAD_DIM
    tile = y[:, width:].astype(jnp.float32)
    lane = lax.broadcasted_iota(jnp.int32, tile.shape, 1)
    kept = jnp.logical_or(lane < 16, jnp.logical_and(lane >= 64, lane < 80))
    stats = jnp.where(kept, tile + pltpu.roll(tile, LANES - 16, 1), 0.0)
    pieces = []
    for j in range(heads):
        v = y[:, j * HEAD_DIM : (j + 1) * HEAD_DIM].astype(jnp.float32)
        size = jnp.log(jnp.abs(v)) * (1.0 / (SPREAD * math.log(2.0))) + 0.5
        size = size * tile[:, 32 + j : 33 + j]
        pieces.append(jnp.where(v < 0.0, -size, size))
    pieces.append(stats)
    return jnp.concatenate(pieces, axis=1)


def merge(x, y, heads):
    width = heads * HEAD_DIM
    sx, sy = x[:, width:], y[:, width:]
    top = jnp.maximum(sx, sy)
    fx, fy = jnp.exp2(sx - top), jnp.exp2(sy - top)
    lane = lax.broadcasted_iota(jnp.int32, sx.shape, 1)
    den = sx * pltpu.roll(fx, 64, 1) + sy * pltpu.roll(fy, 64, 1)
    pieces = []
    for j in range(heads):
        cut = slice(j * HEAD_DIM, (j + 1) * HEAD_DIM)
        pieces.append(x[:, cut] * fx[:, j : j + 1] + y[:, cut] * fy[:, j : j + 1])
    pieces.append(jnp.where(lane < 64, top, den))
    return jnp.concatenate(pieces, axis=1)


def kernel(
    n, chunks,
    tok_ref, start_ref, q_ref, k_hbm, v_hbm, sk_ref, sv_ref, o_ref,
    qg, kbuf, vbuf, part, ea, eb, ec, ra, rb, rc, bias_row, bias_span,
    kv_sem, g_send, g_recv, a_send, a_recv, b_send, b_recv, c_send, c_recv,
):
    rows, width = k_hbm.shape
    own = q_ref.shape[0]
    halves = qg.shape[0]
    chips = n // 2
    far = chips // 2
    total = n * own
    heads = width // HEAD_DIM // chunks
    cw = heads * HEAD_DIM
    cs = cw + LANES
    coef = math.log2(math.e) / math.sqrt(HEAD_DIM)

    me = lax.axis_index("seq")
    group = lax.axis_index("groups")
    core = lax.rem(me, 2)
    side = lax.rem(me // 2, 2)
    hi = me // 4

    def device(hi_, side_, core_):
        return (group, (hi_ * 2 + side_) * 2 + core_)

    def slot_of(hi_, side_, core_):
        return core_ * chips + side_ * far + hi_

    sibling = device(hi, side, 1 - core)
    across = device(hi, 1 - side, core)

    def kv_copy(c, which):
        cut = pl.ds(pl.multiple_of(c * cw, LANES), cw)
        src, dst = (k_hbm, kbuf) if which == 0 else (v_hbm, vbuf)
        return pltpu.make_async_copy(
            src.at[:, cut], dst.at[pl.ds(0, rows), cut], kv_sem.at[which, c]
        )

    for c in range(chunks):
        kv_copy(c, 0).start()
        kv_copy(c, 1).start()

    barrier = pltpu.get_barrier_semaphore()
    pl.semaphore_signal(barrier, inc=1, device_id=sibling, device_id_type=MESH)
    pl.semaphore_signal(barrier, inc=1, device_id=across, device_id_type=MESH)
    for d in range(1, far):
        pl.semaphore_signal(
            barrier, inc=1, device_id=device(lax.rem(hi + d, far), side, core), device_id_type=MESH
        )

    my_slot = slot_of(hi, side, core)
    half_width = width // halves
    for g in range(halves):
        qg[g, pl.ds(my_slot, 1)] = q_ref[:, g * half_width : (g + 1) * half_width][None]

    pl.semaphore_wait(barrier, far + 1)

    def gather_copy(g, slot, to, number):
        return pltpu.make_async_remote_copy(
            src_ref=qg.at[g, slot], dst_ref=qg.at[g, slot],
            send_sem=g_send.at[g, number], recv_sem=g_recv.at[g, slot],
            device_id=to, device_id_type=MESH,
        )

    def from_behind(d):
        return lax.rem(hi - d + far, far)

    def gather_wait(g, slot):
        gather_copy(g, slot, sibling, 0).wait_recv()

    def gather_own(g):
        for d in range(1, far):
            to = device(lax.rem(hi + d, far), side, core)
            gather_copy(g, my_slot, to, d - 1).start()
        gather_copy(g, my_slot, across, far - 1).start()
        gather_copy(g, my_slot, sibling, 2 * far - 1).start()

    def gather_far(g):
        for d in range(1, far):
            slot = slot_of(from_behind(d), side, core)
            gather_wait(g, slot)
            gather_copy(g, slot, across, far - 1 + d).start()
            gather_copy(g, slot, sibling, 2 * far - 1 + d).start()

    def gather_across(g):
        for d in range(far):
            slot = slot_of(from_behind(d), 1 - side, core)
            gather_wait(g, slot)
            gather_copy(g, slot, sibling, 3 * far - 1 + d).start()

    def gather_sibling(g):
        for s_side in (side, 1 - side):
            for d in range(far):
                gather_wait(g, slot_of(from_behind(d), s_side, 1 - core))

    for g in range(halves):
        gather_own(g)

    position = me * rows + lax.broadcasted_iota(jnp.int32, bias_row.shape, 1)
    bias_row[...] = jnp.where(position < tok_ref[0], 0.0, NEG_FILL)
    shape = (total, LANES)
    row = lax.broadcasted_iota(jnp.int32, shape, 0)
    lane = lax.broadcasted_iota(jnp.int32, shape, 1)
    token = row
    for s in range(n):
        s_core, s_side, s_hi = s // chips, (s % chips) // far, s % far
        owner = (s_hi * 2 + s_side) * 2 + s_core
        inside = jnp.logical_and(row >= s * own, row < (s + 1) * own)
        token = jnp.where(inside, row + (owner - s) * own, token)
    key = me * own + lane
    seen = lane < own
    for f in range(1, (FRAME_TOK - 1 + total) // FRAME_TOK + 1):
        edge = f * FRAME_TOK - start_ref[0]
        seen = jnp.logical_and(seen, jnp.logical_or(key < edge, token >= edge))
    bias_span[...] = jnp.where(seen, 0.0, NEG_FILL)
    pad = jnp.zeros((LANES - own, width), jnp.float32)
    for ref, buf in ((sk_ref, kbuf), (sv_ref, vbuf)):
        block = jnp.concatenate([ref[...].astype(jnp.float32), pad], axis=0)
        buf[pl.ds(rows, LANES), :] = block.astype(jnp.bfloat16)

    gather_far(0)
    gather_across(0)
    for g in range(1, halves):
        gather_far(g)
    gather_sibling(0)

    def a_copy(c):
        return pltpu.make_async_remote_copy(
            src_ref=ea.at[c], dst_ref=ra.at[c],
            send_sem=a_send.at[c], recv_sem=a_recv.at[c],
            device_id=sibling, device_id_type=MESH,
        )

    def b_copy(c):
        return pltpu.make_async_remote_copy(
            src_ref=eb.at[c], dst_ref=rb.at[c],
            send_sem=b_send.at[c], recv_sem=b_recv.at[c],
            device_id=across, device_id_type=MESH,
        )

    def c_copy(c, d):
        other = lax.rem(hi + d, far)
        return pltpu.make_async_remote_copy(
            src_ref=ec.at[c, d - 1], dst_ref=rc.at[c, d - 1],
            send_sem=c_send.at[c, d - 1], recv_sem=c_recv.at[c, d - 1],
            device_id=device(other, side, core), device_id_type=MESH,
        )

    def attend(c, first, last):
        stat_lane = lax.broadcasted_iota(jnp.int32, (total, LANES), 1)
        if first == 0:
            stats = jnp.zeros((total, LANES), jnp.float32)
        else:
            stats = part[c, :, :, cw:].reshape(total, LANES)
        per = chunks // halves
        base = lax.rem(c, per) * cw

        def scores(j):
            cut = pl.ds(pl.multiple_of(c * cw + j * HEAD_DIM, LANES), HEAD_DIM)
            q_cut = pl.ds(pl.multiple_of(base + j * HEAD_DIM, LANES), HEAD_DIM)
            q = qg[c // per, :, :, q_cut].astype(jnp.float32).reshape(total, HEAD_DIM)
            s = lax.dot_general(
                q.astype(jnp.bfloat16), kbuf[:, cut], (((1,), (1,)), ((), ())),
                preferred_element_type=jnp.float32,
            ) * coef
            s_cache = s[:, :rows] + bias_row[...]
            s_span = s[:, rows:] + bias_span[...]
            return jnp.concatenate([s_cache, s_span], axis=1)

        ahead = scores(first)
        for j in range(first, last):
            s = ahead
            if j + 1 < last:
                ahead = scores(j + 1)
            cut = pl.ds(pl.multiple_of(c * cw + j * HEAD_DIM, LANES), HEAD_DIM)
            high, low = two_parts(jnp.max(s, axis=1, keepdims=True))
            top = high + low
            w = jnp.exp2(s - top)
            den = jnp.sum(w, axis=1, keepdims=True)
            num = jnp.dot(w.astype(jnp.bfloat16), vbuf[:, cut], preferred_element_type=jnp.float32)
            part[c, :, :, j * HEAD_DIM : (j + 1) * HEAD_DIM] = num.reshape(n, own, HEAD_DIM)
            stats = jnp.where(stat_lane == j, top, stats)
            stats = jnp.where(stat_lane == 64 + j, den, stats)
        part[c, :, :, cw:] = stats.reshape(n, own, LANES)

    def merge_a(c):
        a_copy(c).wait_recv()
        mine = pl.ds(core * chips, chips)
        x = part[c, mine].reshape(chips * own, cs)
        x = merge(x, decode(ra[c], heads), heads)
        part[c, mine] = x.reshape(chips, own, cs)
        theirs = part[c, pl.ds(core * chips + (1 - side) * far, far)]
        eb[c] = code(theirs.reshape(far * own, cs), heads)
        b_copy(c).start()

    def merge_b(c):
        b_copy(c).wait_recv()
        mine = pl.ds(core * chips + side * far, far)
        x = part[c, mine].reshape(far * own, cs)
        x = merge(x, decode(rb[c], heads), heads)
        part[c, mine] = x.reshape(far, own, cs)
        for d in range(1, far):
            ec[c, d - 1] = code(part[c, slot_of(lax.rem(hi + d, far), side, core)], heads)
            c_copy(c, d).start()

    def finish(c):
        x = part[c, my_slot]
        for d in range(1, far):
            c_copy(c, d).wait_recv()
            x = merge(x, decode(rc[c, d - 1], heads), heads)
        out = [
            x[:, j * HEAD_DIM : (j + 1) * HEAD_DIM] / x[:, cw + 64 + j : cw + 65 + j]
            for j in range(heads)
        ]
        cut = pl.ds(pl.multiple_of(c * cw, LANES), cw)
        o_ref[:, cut] = jnp.concatenate(out, axis=1).astype(jnp.bfloat16)

    def when(low, t, high, do, c):
        @pl.when(jnp.logical_and(t >= low, t < high))
        def _():
            do(c)

    half = heads // 2

    def open_chunk(c):
        kv_copy(c, 0).wait()
        kv_copy(c, 1).wait()
        attend(c, 0, half)

    def close_chunk(c):
        attend(c, half, heads)
        theirs = part[c, pl.ds((1 - core) * chips, chips)]
        ea[c] = code(theirs.reshape(chips * own, cs), heads)
        a_copy(c).start()

    def step(t, _):
        for g in range(1, halves):
            when(g * (chunks // halves), t, g * (chunks // halves) + 1, gather_sibling, g)
        when(0, t, chunks, open_chunk, t)
        for g in range(1, halves):
            when(0, t, 1, gather_across, g)
        when(1, t, chunks + 1, merge_a, t - 1)
        when(2, t, chunks + 2, merge_b, t - 2)
        when(3, t, chunks + 3, finish, t - 3)
        when(0, t, chunks, close_chunk, t)
        return 0

    lax.fori_loop(0, chunks + 3, step, 0)

    for g in range(halves):
        for number in range(2 * far - 1 + chips):
            gather_copy(g, my_slot, sibling, number).wait_send()
    for c in range(chunks):
        a_copy(c).wait_send()
        b_copy(c).wait_send()
        for d in range(1, far):
            c_copy(c, d).wait_send()


def local(n, queries, cache_keys, cache_values, span_keys, span_values, cache_tokens, span_start):
    own, width = queries.shape
    rows = cache_keys.shape[0]
    heads = width // HEAD_DIM
    chunks = 4 if heads % 4 == 0 else 1
    halves = 2 if chunks % 2 == 0 else 1
    chips = n // 2
    far = chips // 2
    total = n * own
    cs = width // chunks + LANES
    smem = pl.BlockSpec(memory_space=pltpu.SMEM)
    vmem = pl.BlockSpec(memory_space=pltpu.VMEM)
    hbm = pl.BlockSpec(memory_space=pl.ANY)
    dma = pltpu.SemaphoreType.DMA
    return pl.pallas_call(
        functools.partial(kernel, n, chunks),
        out_shape=jax.ShapeDtypeStruct((own, width), jnp.bfloat16),
        in_specs=[smem, smem, vmem, hbm, hbm, vmem, vmem],
        out_specs=vmem,
        scratch_shapes=[
            pltpu.VMEM((halves, n, own, width // halves), jnp.bfloat16),
            pltpu.VMEM((rows + LANES, width), jnp.bfloat16),
            pltpu.VMEM((rows + LANES, width), jnp.bfloat16),
            pltpu.VMEM((chunks, n, own, cs), jnp.float32),
            pltpu.VMEM((chunks, chips * own, cs), jnp.bfloat16),
            pltpu.VMEM((chunks, far * own, cs), jnp.bfloat16),
            pltpu.VMEM((chunks, far - 1, own, cs), jnp.bfloat16),
            pltpu.VMEM((chunks, chips * own, cs), jnp.bfloat16),
            pltpu.VMEM((chunks, far * own, cs), jnp.bfloat16),
            pltpu.VMEM((chunks, far - 1, own, cs), jnp.bfloat16),
            pltpu.VMEM((1, rows), jnp.float32),
            pltpu.VMEM((total, LANES), jnp.float32),
            dma((2, chunks)),
            dma((halves, far - 1 + far + chips)),
            dma((halves, n)),
            dma((chunks,)),
            dma((chunks,)),
            dma((chunks,)),
            dma((chunks,)),
            dma((chunks, far - 1)),
            dma((chunks, far - 1)),
        ],
        compiler_params=pltpu.CompilerParams(
            collective_id=0, has_side_effects=True, vmem_limit_bytes=56 * 1024 * 1024
        ),
    )(cache_tokens, span_start, queries, cache_keys, cache_values, span_keys, span_values)


def solution(mesh):
    placed = (
        P(("groups", "seq"), None),
        P(("groups", "seq"), None),
        P(("groups", "seq"), None),
        P(("groups", "seq"), None),
        P(("groups", "seq"), None),
        P("groups"),
        P("groups"),
    )
    return jax.shard_map(
        functools.partial(local, mesh.shape["seq"]),
        mesh=mesh, in_specs=placed, out_specs=P(("groups", "seq"), None), check_vma=False,
    )
```

```python
import functools
import math

import jax
import jax.numpy as jnp
from jax import lax
from jax.experimental import pallas as pl
from jax.experimental.pallas import tpu as pltpu
from jax.sharding import PartitionSpec as P

HEAD_DIM = 128
FRAME_TOK = 1560
NEG_FILL = -(2.0**100)
SPREAD = 240.0
LANES = 128
MESH = pl.DeviceIdType.MESH


def two_parts(x):
    high = x.astype(jnp.bfloat16).astype(jnp.float32)
    return high, (x - high).astype(jnp.bfloat16).astype(jnp.float32)


def code(x, heads):
    width = heads * HEAD_DIM
    stats = x[:, width:]
    high, low = two_parts(stats)
    tile = high + pltpu.roll(low, 16, 1)
    lane = lax.broadcasted_iota(jnp.int32, stats.shape, 1)
    pieces = []
    for j in range(heads):
        v = x[:, j * HEAD_DIM : (j + 1) * HEAD_DIM]
        size = jnp.abs(v)
        largest = jnp.max(size, axis=1, keepdims=True)
        largest = largest.astype(jnp.bfloat16).astype(jnp.float32)
        y = jnp.exp2(size * (SPREAD / jnp.maximum(largest, 1e-30)) - SPREAD / 2)
        pieces.append(jnp.where(v < 0.0, -y, y).astype(jnp.bfloat16))
        tile = jnp.where(lane == 32 + j, largest, tile)
    pieces.append(tile.astype(jnp.bfloat16))
    return jnp.concatenate(pieces, axis=1)


def decode(y, heads):
    width = heads * HEAD_DIM
    tile = y[:, width:].astype(jnp.float32)
    lane = lax.broadcasted_iota(jnp.int32, tile.shape, 1)
    kept = jnp.logical_or(lane < 16, jnp.logical_and(lane >= 64, lane < 80))
    stats = jnp.where(kept, tile + pltpu.roll(tile, LANES - 16, 1), 0.0)
    pieces = []
    for j in range(heads):
        v = y[:, j * HEAD_DIM : (j + 1) * HEAD_DIM].astype(jnp.float32)
        size = jnp.log(jnp.abs(v)) * (1.0 / (SPREAD * math.log(2.0))) + 0.5
        size = size * tile[:, 32 + j : 33 + j]
        pieces.append(jnp.where(v < 0.0, -size, size))
    pieces.append(stats)
    return jnp.concatenate(pieces, axis=1)


def merge(x, y, heads):
    width = heads * HEAD_DIM
    sx, sy = x[:, width:], y[:, width:]
    top = jnp.maximum(sx, sy)
    fx, fy = jnp.exp2(sx - top), jnp.exp2(sy - top)
    lane = lax.broadcasted_iota(jnp.int32, sx.shape, 1)
    den = sx * pltpu.roll(fx, 64, 1) + sy * pltpu.roll(fy, 64, 1)
    pieces = []
    for j in range(heads):
        cut = slice(j * HEAD_DIM, (j + 1) * HEAD_DIM)
        pieces.append(x[:, cut] * fx[:, j : j + 1] + y[:, cut] * fy[:, j : j + 1])
    pieces.append(jnp.where(lane < 64, top, den))
    return jnp.concatenate(pieces, axis=1)


def kernel(
    n, chunks,
    tok_ref, start_ref, q_ref, k_hbm, v_hbm, sk_ref, sv_ref, o_ref,
    qg, kbuf, vbuf, part, ea, ec, ra, rc, bias_row, bias_span,
    kv_sem, g_send, g_recv, a_send, a_recv, c_send, c_recv,
):
    rows, width = k_hbm.shape
    own = q_ref.shape[0]
    halves = qg.shape[0]
    chips = n // 2
    far = chips // 2
    total = n * own
    heads = width // HEAD_DIM // chunks
    cw = heads * HEAD_DIM
    cs = cw + LANES
    coef = math.log2(math.e) / math.sqrt(HEAD_DIM)

    me = lax.axis_index("seq")
    group = lax.axis_index("groups")
    core = lax.rem(me, 2)
    side = lax.rem(me // 2, 2)
    hi = me // 4

    def device(hi_, side_, core_):
        return (group, (hi_ * 2 + side_) * 2 + core_)

    def slot_of(hi_, side_, core_):
        return core_ * chips + side_ * far + hi_

    sibling = device(hi, side, 1 - core)
    across = device(hi, 1 - side, core)
    partners = (sibling, across, device(hi, 1 - side, 1 - core))

    def kv_copy(c, which):
        cut = pl.ds(pl.multiple_of(c * cw, LANES), cw)
        src, dst = (k_hbm, kbuf) if which == 0 else (v_hbm, vbuf)
        return pltpu.make_async_copy(
            src.at[:, cut], dst.at[pl.ds(0, rows), cut], kv_sem.at[which, c]
        )

    for c in range(chunks):
        kv_copy(c, 0).start()
        kv_copy(c, 1).start()

    barrier = pltpu.get_barrier_semaphore()
    for partner in partners:
        pl.semaphore_signal(barrier, inc=1, device_id=partner, device_id_type=MESH)
    for d in range(1, far):
        pl.semaphore_signal(
            barrier, inc=1, device_id=device(lax.rem(hi + d, far), side, core), device_id_type=MESH
        )

    my_slot = slot_of(hi, side, core)
    half_width = width // halves
    for g in range(halves):
        qg[g, pl.ds(my_slot, 1)] = q_ref[:, g * half_width : (g + 1) * half_width][None]

    pl.semaphore_wait(barrier, far + 2)

    def gather_copy(g, slot, to, number):
        return pltpu.make_async_remote_copy(
            src_ref=qg.at[g, slot], dst_ref=qg.at[g, slot],
            send_sem=g_send.at[g, number], recv_sem=g_recv.at[g, slot],
            device_id=to, device_id_type=MESH,
        )

    def from_behind(d):
        return lax.rem(hi - d + far, far)

    def gather_wait(g, slot):
        gather_copy(g, slot, sibling, 0).wait_recv()

    def gather_own(g):
        for d in range(1, far):
            to = device(lax.rem(hi + d, far), side, core)
            gather_copy(g, my_slot, to, d - 1).start()
        gather_copy(g, my_slot, across, far - 1).start()
        gather_copy(g, my_slot, sibling, 2 * far - 1).start()

    def gather_far(g):
        for d in range(1, far):
            slot = slot_of(from_behind(d), side, core)
            gather_wait(g, slot)
            gather_copy(g, slot, across, far - 1 + d).start()
            gather_copy(g, slot, sibling, 2 * far - 1 + d).start()

    def gather_across(g):
        for d in range(far):
            slot = slot_of(from_behind(d), 1 - side, core)
            gather_wait(g, slot)
            gather_copy(g, slot, sibling, 3 * far - 1 + d).start()

    def gather_sibling(g):
        for s_side in (side, 1 - side):
            for d in range(far):
                gather_wait(g, slot_of(from_behind(d), s_side, 1 - core))

    for g in range(halves):
        gather_own(g)

    position = me * rows + lax.broadcasted_iota(jnp.int32, bias_row.shape, 1)
    bias_row[...] = jnp.where(position < tok_ref[0], 0.0, NEG_FILL)
    shape = (total, LANES)
    row = lax.broadcasted_iota(jnp.int32, shape, 0)
    lane = lax.broadcasted_iota(jnp.int32, shape, 1)
    token = row
    for s in range(n):
        s_core, s_side, s_hi = s // chips, (s % chips) // far, s % far
        owner = (s_hi * 2 + s_side) * 2 + s_core
        inside = jnp.logical_and(row >= s * own, row < (s + 1) * own)
        token = jnp.where(inside, row + (owner - s) * own, token)
    key = me * own + lane
    seen = lane < own
    for f in range(1, (FRAME_TOK - 1 + total) // FRAME_TOK + 1):
        edge = f * FRAME_TOK - start_ref[0]
        seen = jnp.logical_and(seen, jnp.logical_or(key < edge, token >= edge))
    bias_span[...] = jnp.where(seen, 0.0, NEG_FILL)
    pad = jnp.zeros((LANES - own, width), jnp.float32)
    for ref, buf in ((sk_ref, kbuf), (sv_ref, vbuf)):
        block = jnp.concatenate([ref[...].astype(jnp.float32), pad], axis=0)
        buf[pl.ds(rows, LANES), :] = block.astype(jnp.bfloat16)

    gather_far(0)
    gather_across(0)
    for g in range(1, halves):
        gather_far(g)
    gather_sibling(0)

    def a_copy(c, k):
        return pltpu.make_async_remote_copy(
            src_ref=ea.at[c, k], dst_ref=ra.at[c, k],
            send_sem=a_send.at[c, k], recv_sem=a_recv.at[c, k],
            device_id=partners[k], device_id_type=MESH,
        )

    def c_copy(c, d):
        other = lax.rem(hi + d, far)
        return pltpu.make_async_remote_copy(
            src_ref=ec.at[c, d - 1], dst_ref=rc.at[c, d - 1],
            send_sem=c_send.at[c, d - 1], recv_sem=c_recv.at[c, d - 1],
            device_id=device(other, side, core), device_id_type=MESH,
        )

    def attend(c, first, last):
        stat_lane = lax.broadcasted_iota(jnp.int32, (total, LANES), 1)
        if first == 0:
            stats = jnp.zeros((total, LANES), jnp.float32)
        else:
            stats = part[c, :, :, cw:].reshape(total, LANES)
        per = chunks // halves
        base = lax.rem(c, per) * cw

        def scores(j):
            cut = pl.ds(pl.multiple_of(c * cw + j * HEAD_DIM, LANES), HEAD_DIM)
            q_cut = pl.ds(pl.multiple_of(base + j * HEAD_DIM, LANES), HEAD_DIM)
            q = qg[c // per, :, :, q_cut].astype(jnp.float32).reshape(total, HEAD_DIM)
            s = lax.dot_general(
                q.astype(jnp.bfloat16), kbuf[:, cut], (((1,), (1,)), ((), ())),
                preferred_element_type=jnp.float32,
            ) * coef
            s_cache = s[:, :rows] + bias_row[...]
            s_span = s[:, rows:] + bias_span[...]
            return jnp.concatenate([s_cache, s_span], axis=1)

        ahead = scores(first)
        for j in range(first, last):
            s = ahead
            if j + 1 < last:
                ahead = scores(j + 1)
            cut = pl.ds(pl.multiple_of(c * cw + j * HEAD_DIM, LANES), HEAD_DIM)
            high, low = two_parts(jnp.max(s, axis=1, keepdims=True))
            top = high + low
            w = jnp.exp2(s - top)
            den = jnp.sum(w, axis=1, keepdims=True)
            num = jnp.dot(w.astype(jnp.bfloat16), vbuf[:, cut], preferred_element_type=jnp.float32)
            part[c, :, :, j * HEAD_DIM : (j + 1) * HEAD_DIM] = num.reshape(n, own, HEAD_DIM)
            stats = jnp.where(stat_lane == j, top, stats)
            stats = jnp.where(stat_lane == 64 + j, den, stats)
        part[c, :, :, cw:] = stats.reshape(n, own, LANES)

    def merge_near(c):
        for k in range(3):
            a_copy(c, k).wait_recv()
        mine = pl.ds(core * chips + side * far, far)
        x = part[c, mine].reshape(far * own, cs)
        y = decode(ra[c].reshape(3 * far * own, cs), heads)
        cuts = [y[k * far * own : (k + 1) * far * own] for k in range(3)]
        pairs = merge(
            jnp.concatenate([x, cuts[0]], axis=0), jnp.concatenate([cuts[1], cuts[2]], axis=0), heads
        )
        x = merge(pairs[: far * own], pairs[far * own :], heads)
        part[c, mine] = x.reshape(far, own, cs)
        for d in range(1, far):
            ec[c, d - 1] = code(part[c, slot_of(lax.rem(hi + d, far), side, core)], heads)
            c_copy(c, d).start()

    def finish(c):
        x = part[c, my_slot]
        for d in range(1, far):
            c_copy(c, d).wait_recv()
            x = merge(x, decode(rc[c, d - 1], heads), heads)
        out = [
            x[:, j * HEAD_DIM : (j + 1) * HEAD_DIM] / x[:, cw + 64 + j : cw + 65 + j]
            for j in range(heads)
        ]
        cut = pl.ds(pl.multiple_of(c * cw, LANES), cw)
        o_ref[:, cut] = jnp.concatenate(out, axis=1).astype(jnp.bfloat16)

    def when(low, t, high, do, c):
        @pl.when(jnp.logical_and(t >= low, t < high))
        def _():
            do(c)

    half = heads // 2

    def open_chunk(c):
        kv_copy(c, 0).wait()
        kv_copy(c, 1).wait()
        attend(c, 0, half)

    def close_chunk(c):
        attend(c, half, heads)
        places = ((side, 1 - core), (1 - side, core), (1 - side, 1 - core))
        for k, (side_, core_) in enumerate(places):
            theirs = part[c, pl.ds(core_ * chips + side_ * far, far)]
            ea[c, k] = code(theirs.reshape(far * own, cs), heads)
            a_copy(c, k).start()

    def step(t, _):
        for g in range(1, halves):
            when(g * (chunks // halves), t, g * (chunks // halves) + 1, gather_sibling, g)
        when(0, t, chunks, open_chunk, t)
        for g in range(1, halves):
            when(0, t, 1, gather_across, g)
        when(0, t, chunks, close_chunk, t)
        when(1, t, chunks + 1, merge_near, t - 1)
        when(2, t, chunks + 2, finish, t - 2)
        return 0

    lax.fori_loop(0, chunks + 2, step, 0)

    for g in range(halves):
        for number in range(2 * far - 1 + chips):
            gather_copy(g, my_slot, sibling, number).wait_send()
    for c in range(chunks):
        for k in range(3):
            a_copy(c, k).wait_send()
        for d in range(1, far):
            c_copy(c, d).wait_send()


def local(n, queries, cache_keys, cache_values, span_keys, span_values, cache_tokens, span_start):
    own, width = queries.shape
    rows = cache_keys.shape[0]
    heads = width // HEAD_DIM
    chunks = 4 if heads % 4 == 0 else 1
    halves = 2 if chunks % 2 == 0 else 1
    chips = n // 2
    far = chips // 2
    total = n * own
    cs = width // chunks + LANES
    smem = pl.BlockSpec(memory_space=pltpu.SMEM)
    vmem = pl.BlockSpec(memory_space=pltpu.VMEM)
    hbm = pl.BlockSpec(memory_space=pl.ANY)
    dma = pltpu.SemaphoreType.DMA
    return pl.pallas_call(
        functools.partial(kernel, n, chunks),
        out_shape=jax.ShapeDtypeStruct((own, width), jnp.bfloat16),
        in_specs=[smem, smem, vmem, hbm, hbm, vmem, vmem],
        out_specs=vmem,
        scratch_shapes=[
            pltpu.VMEM((halves, n, own, width // halves), jnp.bfloat16),
            pltpu.VMEM((rows + LANES, width), jnp.bfloat16),
            pltpu.VMEM((rows + LANES, width), jnp.bfloat16),
            pltpu.VMEM((chunks, n, own, cs), jnp.float32),
            pltpu.VMEM((chunks, 3, far * own, cs), jnp.bfloat16),
            pltpu.VMEM((chunks, far - 1, own, cs), jnp.bfloat16),
            pltpu.VMEM((chunks, 3, far * own, cs), jnp.bfloat16),
            pltpu.VMEM((chunks, far - 1, own, cs), jnp.bfloat16),
            pltpu.VMEM((1, rows), jnp.float32),
            pltpu.VMEM((total, LANES), jnp.float32),
            dma((2, chunks)),
            dma((halves, far - 1 + far + chips)),
            dma((halves, n)),
            dma((chunks, 3)),
            dma((chunks, 3)),
            dma((chunks, far - 1)),
            dma((chunks, far - 1)),
        ],
        compiler_params=pltpu.CompilerParams(
            collective_id=0, has_side_effects=True, vmem_limit_bytes=56 * 1024 * 1024
        ),
    )(cache_tokens, span_start, queries, cache_keys, cache_values, span_keys, span_values)


def solution(mesh):
    placed = (
        P(("groups", "seq"), None),
        P(("groups", "seq"), None),
        P(("groups", "seq"), None),
        P(("groups", "seq"), None),
        P(("groups", "seq"), None),
        P("groups"),
        P("groups"),
    )
    return jax.shard_map(
        functools.partial(local, mesh.shape["seq"]),
        mesh=mesh, in_specs=placed, out_specs=P(("groups", "seq"), None), check_vma=False,
    )
```

```python
import functools
import math

import jax
import jax.numpy as jnp
from jax import lax
from jax.experimental import pallas as pl
from jax.experimental.pallas import tpu as pltpu
from jax.sharding import PartitionSpec as P

HEAD_DIM = 128
FRAME_TOK = 1560
NEG_FILL = -(2.0**100)
SPREAD = 240.0
LANES = 128
MESH = pl.DeviceIdType.MESH


def two_parts(x):
    high = x.astype(jnp.bfloat16).astype(jnp.float32)
    return high, (x - high).astype(jnp.bfloat16).astype(jnp.float32)


def code(x, heads):
    width = heads * HEAD_DIM
    stats = x[:, width:]
    high, low = two_parts(stats)
    tile = high + pltpu.roll(low, 16, 1)
    lane = lax.broadcasted_iota(jnp.int32, stats.shape, 1)
    pieces = []
    for j in range(heads):
        v = x[:, j * HEAD_DIM : (j + 1) * HEAD_DIM]
        size = jnp.abs(v)
        largest = jnp.max(size, axis=1, keepdims=True)
        largest = largest.astype(jnp.bfloat16).astype(jnp.float32)
        y = jnp.exp2(size * (SPREAD / jnp.maximum(largest, 1e-30)) - SPREAD / 2)
        pieces.append(jnp.where(v < 0.0, -y, y).astype(jnp.bfloat16))
        tile = jnp.where(lane == 32 + j, largest, tile)
    pieces.append(tile.astype(jnp.bfloat16))
    return jnp.concatenate(pieces, axis=1)


def decode(y, heads):
    width = heads * HEAD_DIM
    tile = y[:, width:].astype(jnp.float32)
    lane = lax.broadcasted_iota(jnp.int32, tile.shape, 1)
    kept = jnp.logical_or(lane < 16, jnp.logical_and(lane >= 64, lane < 80))
    stats = jnp.where(kept, tile + pltpu.roll(tile, LANES - 16, 1), 0.0)
    pieces = []
    for j in range(heads):
        v = y[:, j * HEAD_DIM : (j + 1) * HEAD_DIM].astype(jnp.float32)
        size = jnp.log(jnp.abs(v)) * (1.0 / (SPREAD * math.log(2.0))) + 0.5
        size = size * tile[:, 32 + j : 33 + j]
        pieces.append(jnp.where(v < 0.0, -size, size))
    pieces.append(stats)
    return jnp.concatenate(pieces, axis=1)


def merge(x, y, heads):
    width = heads * HEAD_DIM
    sx, sy = x[:, width:], y[:, width:]
    top = jnp.maximum(sx, sy)
    fx, fy = jnp.exp2(sx - top), jnp.exp2(sy - top)
    lane = lax.broadcasted_iota(jnp.int32, sx.shape, 1)
    den = sx * pltpu.roll(fx, 64, 1) + sy * pltpu.roll(fy, 64, 1)
    pieces = []
    for j in range(heads):
        cut = slice(j * HEAD_DIM, (j + 1) * HEAD_DIM)
        pieces.append(x[:, cut] * fx[:, j : j + 1] + y[:, cut] * fy[:, j : j + 1])
    pieces.append(jnp.where(lane < 64, top, den))
    return jnp.concatenate(pieces, axis=1)


def kernel(
    n, chunks,
    tok_ref, start_ref, q_ref, k_hbm, v_hbm, sk_ref, sv_ref, o_ref,
    qg, kbuf, vbuf, part, ea, ec, ra, rc, bias_row, bias_span,
    kv_sem, g_send, g_recv, a_send, a_recv, c_send, c_recv,
):
    rows, width = k_hbm.shape
    own = q_ref.shape[0]
    halves = qg.shape[0]
    chips = n // 2
    far = chips // 2
    total = n * own
    heads = width // HEAD_DIM // chunks
    cw = heads * HEAD_DIM
    cs = cw + LANES
    coef = math.log2(math.e) / math.sqrt(HEAD_DIM)

    me = lax.axis_index("seq")
    group = lax.axis_index("groups")
    core = lax.rem(me, 2)
    side = lax.rem(me // 2, 2)
    hi = me // 4

    def device(hi_, side_, core_):
        return (group, (hi_ * 2 + side_) * 2 + core_)

    def slot_of(hi_, side_, core_):
        return core_ * chips + side_ * far + hi_

    sibling = device(hi, side, 1 - core)
    across = device(hi, 1 - side, core)
    partners = (sibling, across, device(hi, 1 - side, 1 - core))

    def kv_copy(c, which):
        cut = pl.ds(pl.multiple_of(c * cw, LANES), cw)
        src, dst = (k_hbm, kbuf) if which == 0 else (v_hbm, vbuf)
        return pltpu.make_async_copy(
            src.at[:, cut], dst.at[pl.ds(0, rows), cut], kv_sem.at[which, c]
        )

    for c in range(chunks):
        kv_copy(c, 0).start()
        kv_copy(c, 1).start()

    barrier = pltpu.get_barrier_semaphore()
    for partner in partners:
        pl.semaphore_signal(barrier, inc=1, device_id=partner, device_id_type=MESH)
    for d in range(1, far):
        pl.semaphore_signal(
            barrier, inc=1, device_id=device(lax.rem(hi + d, far), side, core), device_id_type=MESH
        )

    my_slot = slot_of(hi, side, core)
    half_width = width // halves
    for g in range(halves):
        qg[g, pl.ds(my_slot, 1)] = q_ref[:, g * half_width : (g + 1) * half_width][None]

    pl.semaphore_wait(barrier, far + 2)

    def gather_copy(g, slot, to, number):
        return pltpu.make_async_remote_copy(
            src_ref=qg.at[g, slot], dst_ref=qg.at[g, slot],
            send_sem=g_send.at[g, number], recv_sem=g_recv.at[g, slot],
            device_id=to, device_id_type=MESH,
        )

    def from_behind(d):
        return lax.rem(hi - d + far, far)

    def gather_wait(g, slot):
        gather_copy(g, slot, sibling, 0).wait_recv()

    def gather_own(g):
        for d in range(1, far):
            to = device(lax.rem(hi + d, far), side, core)
            gather_copy(g, my_slot, to, d - 1).start()
        gather_copy(g, my_slot, across, far - 1).start()
        gather_copy(g, my_slot, sibling, 2 * far - 1).start()

    def gather_far(g):
        for d in range(1, far):
            slot = slot_of(from_behind(d), side, core)
            gather_wait(g, slot)
            gather_copy(g, slot, across, far - 1 + d).start()
            gather_copy(g, slot, sibling, 2 * far - 1 + d).start()

    def gather_across(g):
        for d in range(far):
            slot = slot_of(from_behind(d), 1 - side, core)
            gather_wait(g, slot)
            gather_copy(g, slot, sibling, 3 * far - 1 + d).start()

    def gather_sibling(g):
        for s_side in (side, 1 - side):
            for d in range(far):
                gather_wait(g, slot_of(from_behind(d), s_side, 1 - core))

    for g in range(halves):
        gather_own(g)

    position = me * rows + lax.broadcasted_iota(jnp.int32, bias_row.shape, 1)
    bias_row[...] = jnp.where(position < tok_ref[0], 0.0, NEG_FILL)
    shape = (total, LANES)
    row = lax.broadcasted_iota(jnp.int32, shape, 0)
    lane = lax.broadcasted_iota(jnp.int32, shape, 1)
    token = row
    for s in range(n):
        s_core, s_side, s_hi = s // chips, (s % chips) // far, s % far
        owner = (s_hi * 2 + s_side) * 2 + s_core
        inside = jnp.logical_and(row >= s * own, row < (s + 1) * own)
        token = jnp.where(inside, row + (owner - s) * own, token)
    key = me * own + lane
    seen = lane < own
    for f in range(1, (FRAME_TOK - 1 + total) // FRAME_TOK + 1):
        edge = f * FRAME_TOK - start_ref[0]
        seen = jnp.logical_and(seen, jnp.logical_or(key < edge, token >= edge))
    bias_span[...] = jnp.where(seen, 0.0, NEG_FILL)
    pad = jnp.zeros((LANES - own, width), jnp.float32)
    for ref, buf in ((sk_ref, kbuf), (sv_ref, vbuf)):
        block = jnp.concatenate([ref[...].astype(jnp.float32), pad], axis=0)
        buf[pl.ds(rows, LANES), :] = block.astype(jnp.bfloat16)

    gather_far(0)
    gather_across(0)
    for g in range(1, halves):
        gather_far(g)
    gather_sibling(0)

    def a_copy(c, k):
        return pltpu.make_async_remote_copy(
            src_ref=ea.at[c, k], dst_ref=ra.at[c, k],
            send_sem=a_send.at[c, k], recv_sem=a_recv.at[c, k],
            device_id=partners[k], device_id_type=MESH,
        )

    def c_copy(c, d):
        other = lax.rem(hi + d, far)
        return pltpu.make_async_remote_copy(
            src_ref=ec.at[c, other], dst_ref=rc.at[c, d - 1],
            send_sem=c_send.at[c, d - 1], recv_sem=c_recv.at[c, d - 1],
            device_id=device(other, side, core), device_id_type=MESH,
        )

    def attend(c, first, last):
        stat_lane = lax.broadcasted_iota(jnp.int32, (total, LANES), 1)
        if first == 0:
            stats = jnp.zeros((total, LANES), jnp.float32)
        else:
            stats = part[c, :, :, cw:].reshape(total, LANES)
        per = chunks // halves
        base = lax.rem(c, per) * cw

        def scores(j):
            cut = pl.ds(pl.multiple_of(c * cw + j * HEAD_DIM, LANES), HEAD_DIM)
            q_cut = pl.ds(pl.multiple_of(base + j * HEAD_DIM, LANES), HEAD_DIM)
            q = qg[c // per, :, :, q_cut].astype(jnp.float32).reshape(total, HEAD_DIM)
            s = lax.dot_general(
                q.astype(jnp.bfloat16), kbuf[:, cut], (((1,), (1,)), ((), ())),
                preferred_element_type=jnp.float32,
            ) * coef
            s_cache = s[:, :rows] + bias_row[...]
            s_span = s[:, rows:] + bias_span[...]
            return jnp.concatenate([s_cache, s_span], axis=1)

        ahead = scores(first)
        for j in range(first, last):
            s = ahead
            if j + 1 < last:
                ahead = scores(j + 1)
            cut = pl.ds(pl.multiple_of(c * cw + j * HEAD_DIM, LANES), HEAD_DIM)
            high, low = two_parts(jnp.max(s, axis=1, keepdims=True))
            top = high + low
            w = jnp.exp2(s - top)
            den = jnp.sum(w, axis=1, keepdims=True)
            num = jnp.dot(w.astype(jnp.bfloat16), vbuf[:, cut], preferred_element_type=jnp.float32)
            part[c, :, :, j * HEAD_DIM : (j + 1) * HEAD_DIM] = num.reshape(n, own, HEAD_DIM)
            stats = jnp.where(stat_lane == j, top, stats)
            stats = jnp.where(stat_lane == 64 + j, den, stats)
        part[c, :, :, cw:] = stats.reshape(n, own, LANES)

    def merge_near(c):
        for k in range(3):
            a_copy(c, k).wait_recv()
        mine = pl.ds(core * chips + side * far, far)
        x = part[c, mine].reshape(far * own, cs)
        y = decode(ra[c].reshape(3 * far * own, cs), heads)
        cuts = [y[k * far * own : (k + 1) * far * own] for k in range(3)]
        pairs = merge(
            jnp.concatenate([x, cuts[0]], axis=0), jnp.concatenate([cuts[1], cuts[2]], axis=0), heads
        )
        x = merge(pairs[: far * own], pairs[far * own :], heads)
        part[c, mine] = x.reshape(far, own, cs)
        ec[c] = code(x, heads).reshape(far, own, cs)
        for d in range(1, far):
            c_copy(c, d).start()

    def finish(c):
        x = part[c, my_slot]
        for d in range(1, far):
            c_copy(c, d).wait_recv()
        y = decode(rc[c].reshape((far - 1) * own, cs), heads)
        for d in range(1, far):
            x = merge(x, y[(d - 1) * own : d * own], heads)
        out = [
            x[:, j * HEAD_DIM : (j + 1) * HEAD_DIM] / x[:, cw + 64 + j : cw + 65 + j]
            for j in range(heads)
        ]
        cut = pl.ds(pl.multiple_of(c * cw, LANES), cw)
        o_ref[:, cut] = jnp.concatenate(out, axis=1).astype(jnp.bfloat16)

    def when(low, t, high, do, c):
        @pl.when(jnp.logical_and(t >= low, t < high))
        def _():
            do(c)

    half = heads // 2

    def open_chunk(c):
        kv_copy(c, 0).wait()
        kv_copy(c, 1).wait()
        attend(c, 0, half)

    def close_chunk(c):
        attend(c, half, heads)
        places = ((side, 1 - core), (1 - side, core), (1 - side, 1 - core))
        for k, (side_, core_) in enumerate(places):
            theirs = part[c, pl.ds(core_ * chips + side_ * far, far)]
            ea[c, k] = code(theirs.reshape(far * own, cs), heads)
            a_copy(c, k).start()

    def step(t, _):
        for g in range(1, halves):
            when(g * (chunks // halves), t, g * (chunks // halves) + 1, gather_sibling, g)
        when(0, t, chunks, open_chunk, t)
        for g in range(1, halves):
            when(0, t, 1, gather_across, g)
        when(0, t, chunks, close_chunk, t)
        when(1, t, chunks + 1, merge_near, t - 1)
        when(2, t, chunks + 2, finish, t - 2)
        return 0

    lax.fori_loop(0, chunks + 2, step, 0)

    for g in range(halves):
        for number in range(2 * far - 1 + chips):
            gather_copy(g, my_slot, sibling, number).wait_send()
    for c in range(chunks):
        for k in range(3):
            a_copy(c, k).wait_send()
        for d in range(1, far):
            c_copy(c, d).wait_send()


def local(n, queries, cache_keys, cache_values, span_keys, span_values, cache_tokens, span_start):
    own, width = queries.shape
    rows = cache_keys.shape[0]
    heads = width // HEAD_DIM
    chunks = 4 if heads % 4 == 0 else 1
    halves = 2 if chunks % 2 == 0 else 1
    chips = n // 2
    far = chips // 2
    total = n * own
    cs = width // chunks + LANES
    smem = pl.BlockSpec(memory_space=pltpu.SMEM)
    vmem = pl.BlockSpec(memory_space=pltpu.VMEM)
    hbm = pl.BlockSpec(memory_space=pl.ANY)
    dma = pltpu.SemaphoreType.DMA
    return pl.pallas_call(
        functools.partial(kernel, n, chunks),
        out_shape=jax.ShapeDtypeStruct((own, width), jnp.bfloat16),
        in_specs=[smem, smem, vmem, hbm, hbm, vmem, vmem],
        out_specs=vmem,
        scratch_shapes=[
            pltpu.VMEM((halves, n, own, width // halves), jnp.bfloat16),
            pltpu.VMEM((rows + LANES, width), jnp.bfloat16),
            pltpu.VMEM((rows + LANES, width), jnp.bfloat16),
            pltpu.VMEM((chunks, n, own, cs), jnp.float32),
            pltpu.VMEM((chunks, 3, far * own, cs), jnp.bfloat16),
            pltpu.VMEM((chunks, far, own, cs), jnp.bfloat16),
            pltpu.VMEM((chunks, 3, far * own, cs), jnp.bfloat16),
            pltpu.VMEM((chunks, far - 1, own, cs), jnp.bfloat16),
            pltpu.VMEM((1, rows), jnp.float32),
            pltpu.VMEM((total, LANES), jnp.float32),
            dma((2, chunks)),
            dma((halves, far - 1 + far + chips)),
            dma((halves, n)),
            dma((chunks, 3)),
            dma((chunks, 3)),
            dma((chunks, far - 1)),
            dma((chunks, far - 1)),
        ],
        compiler_params=pltpu.CompilerParams(
            collective_id=0, has_side_effects=True, vmem_limit_bytes=56 * 1024 * 1024
        ),
    )(cache_tokens, span_start, queries, cache_keys, cache_values, span_keys, span_values)


def solution(mesh):
    placed = (
        P(("groups", "seq"), None),
        P(("groups", "seq"), None),
        P(("groups", "seq"), None),
        P(("groups", "seq"), None),
        P(("groups", "seq"), None),
        P("groups"),
        P("groups"),
    )
    return jax.shard_map(
        functools.partial(local, mesh.shape["seq"]),
        mesh=mesh, in_specs=placed, out_specs=P(("groups", "seq"), None), check_vma=False,
    )
```
